256 devices in a mesh: section: 2 (over core), fsdp: 2 (over z_lo), tok: 64 (over x, z_hi, y).
Axes of the slice: x: 4, y: 4, z: 8 (z_hi: 4, z_lo: 2; z = z_hi * 2 + z_lo), core: 2. Of those that a mesh axis runs over, the one named last changes fastest.
Arguments:
- hidden: bfloat16 [4, 256, 3072], P(None, 'tok'), may hold values from -6 to 6
- lengths: int32 [4], replicated, may hold values from 1 to 256, 768 in all
- text_count: int32 [1], replicated, may hold values from 1 to 256
- timestep: int32 [1], replicated, may hold values from 0 to 49
- mod_table: bfloat16 [2, 50, 6, 3072], P('section'), may hold values from -3 to 3
- w_qkv: bfloat16 [2, 3072, 3, 1536], P('section', 'tok', None, 'fsdp'), may hold values from -0.109375 to 0.109375
- w_out: bfloat16 [2, 3072, 1536], P('section', 'tok', 'fsdp'), may hold values from -0.15625 to 0.15625
- qk_gain: float32 [2, 2, 64], P('section'), may hold values from 0.5 to 2
- stale_cache: bfloat16 [2, 2, 4, 256, 1536], P('section', None, None, None, 'fsdp'), may hold values from -6 to 6
Outputs:
- layer_out: bfloat16 [2, 4, 256, 3072], P('section', None, 'tok')
- new_cache: bfloat16 [2, 2, 4, 256, 1536], P('section', None, None, None, 'fsdp')
The draws below stay inside these ranges and needn't reach their ends.
Inputs may be any that keep to these rules, and one draw needn't show every extreme that they name: The lengths sum to 768; one patch is full with exactly 256 live tokens.
All inputs are finite; a program needn't handle non-finite values.
Results may differ from the reference program's by a relative error of at most 0.012.
Values may be sent and summed in bfloat16 or wider, within the bound.
A program may use at most 128 MiB of HBM per device.

```python
import math
import jax
import jax.numpy as jnp
import numpy as np
from jax import lax

D = 3072
HEADS = 24
HEAD_DIM = 64
PATCHES = 4
STEPS = 50
HD = 1536
CAP = 256
LIVE = 768
SECTIONS = 2


def block_scale(key, dims, cuts, smallest, largest):
    gain, own = 1.0, jax.random.fold_in(key, 6)
    for axis_at, parts in cuts:
        heights = jnp.exp(jax.random.uniform(jax.random.fold_in(own, axis_at), (parts,), jnp.float32, smallest / len(cuts), largest / len(cuts)))
        gain = gain * jnp.repeat(heights, dims[axis_at] // parts).reshape([-1 if axis == axis_at else 1 for axis in range(len(dims))])
    return gain


def split_up(number_of, total, limit, skew):
    loads = [(1 << 20) // math.isqrt(rank ** skew) + 1 for rank in range(2, number_of + 1)]
    rest, counts = total - limit - (number_of - 1), [1] * (number_of - 1)
    while rest > 0:
        free = [i for i in range(number_of - 1) if counts[i] < limit]
        whole, remaining = sum([loads[i] for i in free]), rest
        for i in free:
            more = min(limit - counts[i], max(1, remaining * loads[i] // whole), rest)
            counts[i] = counts[i] + more
            rest = rest - more
    return np.array([limit] + counts)


def uneven_parts(key, number_of, total, limit, skew):
    if number_of == 2:
        one = jax.random.randint(key, (), max(1, total - limit), min(limit, total - 1) + 1)
        return jnp.stack([one, total - one])
    tallies = jnp.asarray(split_up(number_of, total, limit, skew), jnp.int32)
    pairs = (number_of - 1) // 2
    source_of, sink = tallies[1:1 + 2 * pairs:2], tallies[2:2 + 2 * pairs:2]
    slack = jnp.minimum(source_of - 1, limit - sink)
    moved = jax.random.randint(jax.random.fold_in(key, 1), (pairs,), 0, 1 << 20) % (slack + 1)
    tallies = tallies.at[1:1 + 2 * pairs:2].set(source_of - moved).at[2:2 + 2 * pairs:2].set(sink + moved)
    return tallies[jax.random.permutation(jax.random.fold_in(key, 2), number_of)]


def gaussian(rng, shape, scale, reach, cuts=(), kind=jnp.bfloat16):
    drawn = scale * jax.random.normal(rng, shape, jnp.float32)
    if cuts:
        drawn = drawn * block_scale(rng, shape, cuts, -0.22, 0.18)
    return jnp.clip(drawn, -reach, reach).astype(kind)


def setup_inputs(seed: int = 0) -> dict:
    splits = jax.random.split(jax.random.key(seed), 10)
    return {
        "hidden": gaussian(splits[0], (PATCHES, CAP, D), 1.0, 6.0, ((1, 64),)),
        "lengths": uneven_parts(splits[1], PATCHES, LIVE, CAP, 0).astype(jnp.int32),
        "text_count": jax.random.randint(splits[2], (1,), 1, CAP + 1).astype(jnp.int32),
        "timestep": jax.random.randint(splits[3], (1,), 0, STEPS).astype(jnp.int32),
        "mod_table": gaussian(splits[4], (SECTIONS, STEPS, 6, D), 0.5, 3.0, ((0, 2),)),
        "w_qkv": gaussian(splits[5], (SECTIONS, D, 3, HD), D ** -0.5, 0.109375, ((0, 2), (1, 64), (3, 2))),
        "w_out": gaussian(splits[6], (SECTIONS, D, HD), HD ** -0.5, 0.15625, ((0, 2), (1, 64), (2, 2))),
        "qk_gain": jnp.clip(jnp.exp(math.log(2.0) - 1.3862944 * jax.random.uniform(splits[7], (SECTIONS, 2, HEAD_DIM), jnp.float32) ** block_scale(splits[7], (SECTIONS, 2, HEAD_DIM), ((0, 2),), -0.2, 0.2)), 0.5, 2.0),
        "stale_cache": gaussian(splits[8], (SECTIONS, 2, PATCHES, CAP, HD), 1.0, 6.0, ((0, 2), (4, 2))),
    }


def layer_norm(values, eps):
    mean = lax.optimization_barrier(jnp.mean(values, axis=-1, keepdims=True))
    centred = values - mean
    spread = lax.optimization_barrier(jnp.mean(centred * centred, axis=-1, keepdims=True))
    return centred * lax.rsqrt(spread + eps)

def modulate(inputs, positions, modulation, text_total):
    is_text = (positions < text_total)[:, None]
    shift = jnp.where(is_text, modulation[3], modulation[0])
    scale = jnp.where(is_text, modulation[4], modulation[1])
    gate = jnp.where(is_text, modulation[5], modulation[2])
    normed = layer_norm(inputs, 1e-05)
    return ((normed * (1.0 + scale) + shift).astype(jnp.bfloat16), gate)

def project_heads(mixed, gains):
    queries = (layer_norm(mixed[:, 0], 1e-06) * gains[0]).astype(jnp.bfloat16)
    keys_new = (layer_norm(mixed[:, 1], 1e-06) * gains[1]).astype(jnp.bfloat16)
    values_new = mixed[:, 2].astype(jnp.bfloat16)
    return (queries, keys_new, values_new)

def attend(queries, keys_all, values_all, key_live):
    scores = jnp.einsum('qhd,khd->hqk', queries.astype(jnp.float32), keys_all.astype(jnp.float32)) * HEAD_DIM ** (-0.5)
    scores = jnp.where(key_live[None, None, :], scores, -jnp.inf)
    top = lax.optimization_barrier(jnp.max(scores, axis=-1, keepdims=True))
    expo = jnp.exp(scores - top)
    weights = (expo / lax.optimization_barrier(jnp.sum(expo, axis=-1, keepdims=True))).astype(jnp.bfloat16)
    return jnp.einsum('hqk,khd->qhd', weights.astype(jnp.float32), values_all.astype(jnp.float32)).astype(jnp.bfloat16)

def reference(hidden, lengths, text_count, timestep, mod_table, w_qkv, w_out, qk_gain, stale_cache):
    offsets = jnp.cumsum(lengths) - lengths
    slots = jnp.arange(CAP, dtype=jnp.int32)
    key_live = (slots[None, :] < lengths[:, None]).reshape(-1)
    section_in = hidden
    outputs = []
    caches = []
    for section in range(SECTIONS):
        modulation = lax.dynamic_index_in_dim(mod_table[section], timestep[0], 0, keepdims=False).astype(jnp.float32)
        weight_in = w_qkv[section].reshape(D, 3 * HD)
        cache_keys = stale_cache[section, 0].reshape(PATCHES, CAP, HEADS, HEAD_DIM)
        cache_values = stale_cache[section, 1].reshape(PATCHES, CAP, HEADS, HEAD_DIM)
        results = []
        for patch in range(PATCHES):
            inputs = section_in[patch].astype(jnp.float32)
            row_live = slots < lengths[patch]
            modded, gate = modulate(inputs, offsets[patch] + slots, modulation, text_count[0])
            mixed = jnp.dot(modded, weight_in, preferred_element_type=jnp.float32).reshape(CAP, 3, HEADS, HEAD_DIM)
            queries, keys_new, values_new = project_heads(mixed, qk_gain[section])
            keys_new = jnp.where(row_live[:, None, None], keys_new, jnp.zeros_like(keys_new))
            values_new = jnp.where(row_live[:, None, None], values_new, jnp.zeros_like(values_new))
            cache_keys = cache_keys.at[patch].set(keys_new)
            cache_values = cache_values.at[patch].set(values_new)
            attended = attend(queries, cache_keys.reshape(-1, HEADS, HEAD_DIM), cache_values.reshape(-1, HEADS, HEAD_DIM), key_live).reshape(CAP, HD)
            projected = lax.dot_general(attended, w_out[section], (((1,), (1,)), ((), ())), preferred_element_type=jnp.float32)
            result = jnp.where(row_live[:, None], inputs + gate * projected, 0.0).astype(jnp.bfloat16)
            results.append(result)
        section_in = jnp.stack(results)
        outputs.append(section_in)
        caches.append(jnp.stack([cache_keys.reshape(PATCHES, CAP, HD), cache_values.reshape(PATCHES, CAP, HD)]))
    return (jnp.stack(outputs), jnp.stack(caches))
```

```python
import functools

import jax
import jax.numpy as jnp
from jax import lax
from jax.experimental import pallas as pl
from jax.experimental.pallas import tpu as pltpu
from jax.sharding import PartitionSpec as P

HEAD_DIM = 64
F32 = jnp.float32
BF16 = jnp.bfloat16
HIDE = -1e30
COPIES = 10


def bits(number):
    assert number & (number - 1) == 0
    return number.bit_length() - 1


def matmul(a, b):
    return jnp.dot(a, b, preferred_element_type=F32)


def matmul_t(a, b):
    return lax.dot_general(a, b, (((1,), (1,)), ((), ())), preferred_element_type=F32)


def pick(index, values):
    out = jnp.zeros(index.shape, jnp.int32)
    for at, value in enumerate(values):
        out = jnp.where(index == at, value, out)
    return out


def relay(n, nf, patches, cd, hid, lens, text, mod, wq, wo, gain, stale, lo, cache,
          hmine, hbuf, xb, xs, mb, wmine, wbuf, wobuf, kv, zb, cb, ab, xo, ob, fin, stl, old, sends, recvs, send_w, recv_w, gate):
    width = hid.shape[-1]
    rows_w = wq.shape[0]
    local = wq.shape[2]
    hl = local // n
    hc = hl // HEAD_DIM
    groups = n * n
    ranks = nf * n
    out_w = width // ranks
    run = n * cd
    rows = patches * run
    cap = groups * run
    own_rows = patches * cd

    s, f, t = lax.axis_index("section"), lax.axis_index("fsdp"), lax.axis_index("tok")
    x, z, y = t // (n * n), (t // n) % n, t % n
    g = x * n + y
    k = f * n + z

    def to(x_, z_, y_, f_=None, s_=None):
        return {"section": s if s_ is None else s_, "fsdp": f if f_ is None else f_, "tok": (x_ * n + z_) * n + y_}

    def remote(src, dst, which, target):
        return pltpu.make_async_remote_copy(
            src_ref=src, dst_ref=dst, send_sem=sends.at[which], recv_sem=recvs.at[which],
            device_id=target, device_id_type=pl.DeviceIdType.MESH)

    def sent(ref, which):
        pltpu.make_async_copy(ref, ref, sends.at[which]).wait()

    def arrived(ref, which):
        pltpu.make_async_copy(ref, ref, recvs.at[which]).wait()

    HID, WA, WO, KV, Z, C, A, X, FIN, STALE = range(COPIES)

    fetch = pltpu.make_async_copy(stale, stl, recvs.at[STALE])
    fetch.start()

    @pl.when(s == 0)
    def _():
        hmine[...] = hid[...].reshape(own_rows, width)

        def send(z_, c):
            same = (z_ == z) & (z == y)

            @pl.when(same)
            def _():
                pltpu.make_async_copy(hmine, hbuf.at[y], recvs.at[HID]).start()

            @pl.when(jnp.logical_not(same))
            def _():
                remote(hmine, hbuf.at[y], HID, to(x, z_, z)).start()
            return c
        lax.fori_loop(0, n, send, 0)

    for z_ in range(n):
        for at, part in enumerate((2, 1, 0)):
            wmine[z_, :, at * hl:(at + 1) * hl] = wq[:, part, z_ * hl:(z_ + 1) * hl]

    def send(d, c):
        z_ = (z + d) % n
        remote(wmine.at[z_], wbuf.at[x, z, y], WA, to(x, z_, y)).start()
        return c
    lax.fori_loop(1, n, send, 0)
    pltpu.make_async_copy(wmine.at[z], wbuf.at[x, z, y], recvs.at[WA]).start()
    arrived(wmine, WA)

    @pl.when(s == 1)
    def _():
        pl.semaphore_wait(gate, 1)

    def send(d, c):
        g_ = (g + d) % groups
        pltpu.make_async_remote_copy(
            src_ref=wbuf.at[x, :, y], dst_ref=wbuf.at[x, :, y], send_sem=send_w.at[g_ // n], recv_sem=recv_w.at[x],
            device_id=to(g_ // n, z, g_ % n), device_id_type=pl.DeviceIdType.MESH).start()
        return c
    lax.fori_loop(1, groups, send, 0)

    per = (n * n * n) // ranks
    kk, place = t // per, t % per
    f_o, z_o = kk // n, kk % n

    def send(g_, c):
        same = (f_o == f) & (z_o == z) & (g_ == g)

        @pl.when(same)
        def _():
            pltpu.make_async_copy(wo, wobuf.at[f * per + place], recvs.at[WO]).start()

        @pl.when(jnp.logical_not(same))
        def _():
            remote(wo, wobuf.at[f * per + place], WO, to(g_ // n, z_o, g_ % n, f_)).start()
        return c
    f_ = f_o
    lax.fori_loop(0, groups, send, 0)

    length = [lens[p] for p in range(patches)]
    start = [sum(length[:p], jnp.int32(0)) for p in range(patches)]

    def about(first, count):
        row = first + lax.broadcasted_iota(jnp.int32, (count, 1), 0)
        row_patch = row >> bits(run)
        slot = g * run + (row & (run - 1))
        return slot < pick(row_patch, length), (pick(row_patch, start) + slot) < text[0]

    live, is_text = about(0, rows)

    r0 = lax.broadcasted_iota(jnp.int32, (rows, rows), 0)
    r1 = lax.broadcasted_iota(jnp.int32, (rows, rows), 1)

    def flipped(r):
        p_, y_, i_ = r >> bits(run), (r >> bits(cd)) & (n - 1), r & (cd - 1)
        return (y_ * patches + p_) * cd + i_

    @pl.when(s == 0)
    def _():
        arrived(hbuf, HID)
        order = (flipped(r0) == r1).astype(BF16)
        xs[...] = matmul(order, hbuf[...].reshape(rows, width)).astype(BF16)

    @pl.when(s == 1)
    def _():
        arrived(xb, X)
        for k_ in range(ranks):
            xs[:, k_ * out_w:(k_ + 1) * out_w] = xb[k_]

    step = min(16, rows)
    for at in range(0, rows, step):
        here = slice(at, at + step)
        values = xs[here, :].astype(F32)
        mean = jnp.mean(values, axis=1, keepdims=True)
        centred = values - mean
        spread = jnp.mean(centred * centred, axis=1, keepdims=True)
        normed = centred * lax.rsqrt(spread + 1e-05)
        text_here = about(at, step)[1]
        scale = jnp.where(text_here, mod[4:5, :], mod[1:2, :])
        shift = jnp.where(text_here, mod[3:4, :], mod[0:1, :])
        mb[here, :] = (normed * (1.0 + scale) + shift).astype(BF16)

    chunk = groups * rows_w
    total = None
    for d in range(n):
        x_ = (x + d) % n
        if d == 0:
            ref = wbuf.at[x_, :, pl.ds(0, n - 1)]
        else:
            ref = wbuf.at[x_]
        pltpu.make_async_copy(ref, ref, recv_w.at[x_]).wait()
        columns = pl.ds(pl.multiple_of(x_ * chunk, chunk), chunk)
        part = matmul(mb[:, columns], wbuf[x_].reshape(chunk, 3 * hl))
        total = part if total is None else total + part

    @pl.when(s == 0)
    def _():
        pl.semaphore_signal(gate, 1, device_id=to(x, z, y, f, 1), device_id_type=pl.DeviceIdType.MESH)

    head = lax.broadcasted_iota(jnp.int32, (1, hl), 1) >> bits(HEAD_DIM)

    def head_norm(values, gains):
        mean = jnp.zeros_like(values)
        for h in range(hc):
            here = head == h
            mean = jnp.where(here, jnp.sum(jnp.where(here, values, 0.0), axis=1, keepdims=True) / HEAD_DIM, mean)
        centred = values - mean
        square = centred * centred
        spread = jnp.zeros_like(values)
        for h in range(hc):
            here = head == h
            spread = jnp.where(here, jnp.sum(jnp.where(here, square, 0.0), axis=1, keepdims=True) / HEAD_DIM, spread)
        return centred * lax.rsqrt(spread + 1e-06) * jnp.concatenate([gains] * hc, axis=1)

    value_new = jnp.where(live, total[:, :hl], 0.0)
    key_new = jnp.where(live, head_norm(total[:, hl:2 * hl], gain[1:2, :]), 0.0)
    query = head_norm(total[:, 2 * hl:], gain[0:1, :])
    kv[g] = jnp.concatenate([value_new, key_new], axis=1).astype(BF16)

    def send(d, c):
        g_ = (g + d) % groups
        remote(kv.at[g], kv.at[g], KV, to(g_ // n, z, g_ % n)).start()
        return c
    lax.fori_loop(1, groups, send, 0)

    def send(d, c):
        z_ = (z + d) % n
        remote(kv.at[g], zb.at[z], Z, to(x, z_, y)).start()
        return c
    lax.fori_loop(1, n, send, 0)
    pltpu.make_async_copy(kv.at[g], zb.at[z], recvs.at[Z]).start()

    query = jnp.concatenate([jnp.zeros((rows, hl), F32), query], axis=1)
    lane = lax.broadcasted_iota(jnp.int32, (1, 2 * hl), 1)
    queries = jnp.concatenate(
        [jnp.where(((lane - hl) >> bits(HEAD_DIM)) == h, query, 0.0) for h in range(hc)], axis=0).astype(BF16)
    query_row = lax.broadcasted_iota(jnp.int32, (hc * rows, 1), 0)
    query_patch = (query_row & (rows - 1)) >> bits(run)
    column = lax.broadcasted_iota(jnp.int32, (1, patches * cap), 1)

    fetch.wait()
    for z_ in range(n):
        @pl.when(z == z_)
        def _(z_=z_):
            mine = slice(z_ * hl, (z_ + 1) * hl)
            both = jnp.concatenate([stl[1, :, :, mine], stl[0, :, :, mine]], axis=2)
            old[...] = both.reshape(patches * cap, 2 * hl)
    old_patch = column >> bits(cap)
    old_seen = ((column & (cap - 1)) < pick(old_patch, length))
    score_old = matmul_t(queries, old[...]) * HEAD_DIM ** (-0.5)
    score_old = jnp.where(old_seen & (old_patch > query_patch), score_old, HIDE)
    top_old = jnp.max(score_old, axis=1, keepdims=True)

    arrived(zb, Z)
    both = jnp.concatenate([zb[z_][:, hl:] for z_ in range(n)], axis=1)
    cb[0] = both.reshape(patches, run, local)
    both = jnp.concatenate([zb[z_][:, :hl] for z_ in range(n)], axis=1)
    cb[1] = both.reshape(patches, run, local)
    spot = pl.ds(pl.multiple_of(g * run, run), run)

    def send(d, c):
        g_ = (g + d) % groups
        remote(cb, cache.at[:, :, spot], C, to(g_ // n, z, g_ % n)).start()
        return c
    lax.fori_loop(1, groups, send, 0)
    pltpu.make_async_copy(cb, cache.at[:, :, spot], recvs.at[C]).start()

    most = kv.at[pl.ds(0, groups - 1)]
    arrived(most, KV)
    new = kv[...].reshape(patches * cap, 2 * hl)
    new_patch = (column >> bits(run)) & (patches - 1)
    new_slot = (column >> bits(rows)) * run + (column & (run - 1))
    new_seen = new_slot < pick(new_patch, length)
    score_new = matmul_t(queries, new) * HEAD_DIM ** (-0.5)
    score_new = jnp.where(new_seen & (new_patch <= query_patch), score_new, HIDE)
    top = jnp.maximum(top_old, jnp.max(score_new, axis=1, keepdims=True))
    expo_old, expo_new = jnp.exp(score_old - top), jnp.exp(score_new - top)
    norm = 1.0 / (jnp.sum(expo_old, axis=1, keepdims=True) + jnp.sum(expo_new, axis=1, keepdims=True))
    taken = matmul((expo_old * norm).astype(BF16), old[...]) + matmul((expo_new * norm).astype(BF16), new)
    attended = jnp.zeros((rows, hl), F32)
    for h in range(hc):
        attended = jnp.where(head == h, taken[h * rows:(h + 1) * rows, :hl], attended)
    ab[k] = attended.astype(BF16)

    def send(d, c):
        k_ = (k + d) % ranks
        remote(ab.at[k], ab.at[k], A, to(x, k_ % n, y, k_ // n)).start()
        return c
    lax.fori_loop(1, ranks, send, 0)

    arrived(wobuf, WO)
    arrived(ab.at[pl.ds(0, ranks - 1)], A)
    projected = None
    for f_ in range(nf):
        left = jnp.concatenate([ab[f_ * n + z_] for z_ in range(n)], axis=1)
        part = matmul_t(left, wobuf[f_ * per:(f_ + 1) * per].reshape(out_w, local))
        projected = part if projected is None else projected + part
    columns = pl.ds(pl.multiple_of(k * out_w, out_w), out_w)
    gated = jnp.where(is_text, mod[5:6, columns], mod[2:3, columns])
    result = jnp.where(live, xs[:, columns].astype(F32) + gated * projected, 0.0).astype(BF16)

    @pl.when(s == 0)
    def _():
        xo[...] = result

        def send(k_, c):
            remote(xo, xb.at[k], X, to(x, k_ % n, y, k_ // n, 1)).start()
            return c
        lax.fori_loop(0, ranks, send, 0)

    back = (r0 == flipped(r1)).astype(BF16)
    ob[...] = matmul(back, result).astype(BF16).reshape(n, own_rows, out_w)

    def send(j, c):
        y_, f_ = j % n, j // n
        same = (y_ == y) & (z == y) & (f_ == f)

        @pl.when(same)
        def _():
            pltpu.make_async_copy(ob.at[y_], fin.at[k], recvs.at[FIN]).start()

        @pl.when(jnp.logical_not(same))
        def _():
            remote(ob.at[y_], fin.at[k], FIN, to(x, y, y_, f_)).start()
        return c
    lax.fori_loop(0, ranks, send, 0)
    arrived(fin, FIN)
    lo[...] = jnp.concatenate([fin[k_] for k_ in range(ranks)], axis=1).reshape(patches, cd, width)
    arrived(cache, C)

    @pl.when(s == 0)
    def _():
        @pl.when(z == y)
        def _():
            sent(hbuf.at[pl.ds(0, n - 1)], HID)

        @pl.when(z != y)
        def _():
            sent(hbuf, HID)
        sent(xb, X)
    sent(wmine.at[pl.ds(0, n - 1)], WA)
    for d in range(n):
        x_ = (x + d) % n
        ref = wbuf.at[x_, :, pl.ds(0, n - 1)] if d == 0 else wbuf.at[x_]
        pltpu.make_async_copy(ref, ref, send_w.at[x_]).wait()
    own_plane = (f_o == f) & (z_o == z)

    @pl.when(own_plane)
    def _():
        sent(wobuf.at[pl.ds(0, groups - 1)], WO)

    @pl.when(jnp.logical_not(own_plane))
    def _():
        sent(wobuf, WO)
    sent(most, KV)
    sent(zb.at[pl.ds(0, n - 1)], Z)
    sent(cache.at[:, :, pl.ds(0, (groups - 1) * run)], C)
    sent(ab.at[pl.ds(0, ranks - 1)], A)

    @pl.when(z == y)
    def _():
        sent(fin.at[pl.ds(0, ranks - 1)], FIN)

    @pl.when(z != y)
    def _():
        sent(fin, FIN)


def local(n, hidden, lengths, text_count, timestep, mod_table, w_qkv, w_out, qk_gain, stale_cache):
    nf = lax.axis_size("fsdp")
    patches, cd, width = hidden.shape
    rows_w, local_width = w_qkv.shape[1], w_qkv.shape[3]
    hl, groups, ranks = local_width // n, n * n, nf * n
    run = n * cd
    rows, out_w, own_rows, cap = patches * run, width // ranks, patches * cd, groups * run
    per = n * n * n // ranks
    mod = lax.dynamic_index_in_dim(mod_table[0], timestep[0], 0, keepdims=False).astype(F32)
    vmem, smem, anywhere = (pl.BlockSpec(memory_space=m) for m in (pltpu.VMEM, pltpu.SMEM, pl.ANY))
    out, cache = pl.pallas_call(
        functools.partial(relay, n, nf, patches, cd),
        out_shape=(
            jax.ShapeDtypeStruct((patches, cd, width), BF16),
            jax.ShapeDtypeStruct((2, patches, cap, local_width), BF16),
        ),
        in_specs=[vmem, smem, smem, vmem, vmem, vmem, vmem, anywhere],
        out_specs=(vmem, anywhere),
        scratch_shapes=[
            pltpu.VMEM((own_rows, width), BF16),
            pltpu.VMEM((n, own_rows, width), BF16),
            pltpu.VMEM((ranks, rows, out_w), BF16),
            pltpu.VMEM((rows, width), BF16),
            pltpu.VMEM((rows, width), BF16),
            pltpu.VMEM((n, rows_w, 3 * hl), BF16),
            pltpu.VMEM((n, n, n, rows_w, 3 * hl), BF16),
            pltpu.VMEM((nf * per, rows_w, local_width), BF16),
            pltpu.VMEM((groups, rows, 2 * hl), BF16),
            pltpu.VMEM((n, rows, 2 * hl), BF16),
            pltpu.VMEM((2, patches, run, local_width), BF16),
            pltpu.VMEM((ranks, rows, hl), BF16),
            pltpu.VMEM((rows, out_w), BF16),
            pltpu.VMEM((n, own_rows, out_w), BF16),
            pltpu.VMEM((ranks, own_rows, out_w), BF16),
            pltpu.VMEM((2, patches, cap, local_width), BF16),
            pltpu.VMEM((patches * cap, 2 * hl), BF16),
            pltpu.SemaphoreType.DMA((COPIES,)),
            pltpu.SemaphoreType.DMA((COPIES,)),
            pltpu.SemaphoreType.DMA((n,)),
            pltpu.SemaphoreType.DMA((n,)),
            pltpu.SemaphoreType.REGULAR,
        ],
        compiler_params=pltpu.CompilerParams(has_side_effects=True, vmem_limit_bytes=48 * 2**20),
    )(hidden, lengths, text_count, mod, w_qkv[0], w_out[0], qk_gain[0], stale_cache[0])
    return out[None], cache[None]


def solution(mesh):
    n = round(mesh.shape["tok"] ** (1 / 3))
    in_specs = (
        P(None, "tok", None),
        P(),
        P(),
        P(),
        P("section", None, None, None),
        P("section", "tok", None, "fsdp"),
        P("section", "tok", "fsdp"),
        P("section", None, None),
        P("section", None, None, None, "fsdp"),
    )
    out_specs = (P("section", None, "tok", None), P("section", None, None, None, "fsdp"))
    return jax.shard_map(
        functools.partial(local, n), mesh=mesh, in_specs=in_specs, out_specs=out_specs, check_vma=False
    )
```

```python
import functools

import jax
import jax.numpy as jnp
from jax import lax
from jax.experimental import pallas as pl
from jax.experimental.pallas import tpu as pltpu
from jax.sharding import PartitionSpec as P

HEAD_DIM = 64
F32 = jnp.float32
BF16 = jnp.bfloat16
HIDE = -1e30
HID, WA, KV, Z, A, F, X, FIN = range(8)
COPIES = 8
FETCHES = 7


def bits(number):
    assert number & (number - 1) == 0
    return number.bit_length() - 1


def matmul(a, b):
    return jnp.dot(a, b, preferred_element_type=F32)


def matmul_t(a, b):
    return lax.dot_general(a, b, (((1,), (1,)), ((), ())), preferred_element_type=F32)


def pick(index, values):
    out = jnp.zeros(index.shape, jnp.int32)
    for at, value in enumerate(values):
        out = jnp.where(index == at, value, out)
    return out


def relay(n, nf, patches, cd, hid_in, lens_in, text_in, time_in, mod_in, wq_in, wo_in, gain, stale, lo, cache,
          lens, text, time, hid, hmine, hbuf, xb, mod_all, mod, mb, wq, wmine, wbuf, wobuf, kv, zb, cb, ab, osum, osend,
          orecv, ob, fin, stl, old, fetches, sends, recvs, first, second, out_first, out_second, gate):
    width = hid.shape[-1]
    rows_w = wq.shape[1]
    local = wq.shape[2]
    hl = local // n
    hc = hl // HEAD_DIM
    groups = n * n
    ranks = nf * n
    out_w = width // ranks
    run = n * cd
    rows = patches * run
    cap = groups * run
    own_rows = patches * cd
    piece = width // groups

    s, f, t = lax.axis_index("section"), lax.axis_index("fsdp"), lax.axis_index("tok")
    x, z, y = t // (n * n), (t // n) % n, t % n
    g = x * n + y
    k = z * nf + f

    def to(x_, z_, y_, f_=None, s_=None):
        return {"section": s if s_ is None else s_, "fsdp": f if f_ is None else f_, "tok": (x_ * n + z_) * n + y_}

    def copy_to(src, dst, send, recv, target):
        return pltpu.make_async_remote_copy(
            src_ref=src, dst_ref=dst, send_sem=send, recv_sem=recv, device_id=target,
            device_id_type=pl.DeviceIdType.MESH)

    def remote(src, dst, which, target):
        return copy_to(src, dst, sends.at[which], recvs.at[which], target)

    def settle(ref, sem):
        pltpu.make_async_copy(ref, ref, sem).wait()

    def sent(ref, which):
        settle(ref, sends.at[which])

    def arrived(ref, which):
        settle(ref, recvs.at[which])

    def loop(low, high, body):
        def step(i, c):
            body(i)
            return c
        lax.fori_loop(low, high, step, 0)

    fetched = [pltpu.make_async_copy(a, b, fetches.at[i]) for i, (a, b) in enumerate(
        ((hid_in, hid), (wq_in, wq), (lens_in, lens), (text_in, text), (time_in, time), (mod_in, mod_all), (stale, stl)))]
    for fetch in fetched:
        fetch.start()

    barrier = pltpu.get_barrier_semaphore()

    def greet(target):
        pl.semaphore_signal(barrier, inc=1, device_id=target, device_id_type=pl.DeviceIdType.MESH)

    def greet_plane(d):
        g_ = (g + d) % groups
        greet(to(g_ // n, z, g_ % n))
    loop(1, groups, greet_plane)

    def greet_ring(d):
        k_ = (k + d) % ranks
        greet(to(x, k_ // nf, y, k_ % nf))
    loop(1, ranks, greet_ring)

    def greet_section(k_):
        greet(to(x, k_ // nf, y, k_ % nf, 1 - s))
    loop(0, ranks, greet_section)

    def greet_owner(j):
        j_, f_ = j // nf, j % nf

        @pl.when(jnp.logical_not((z == y) & (j_ == z) & (f_ == f)))
        def _():
            greet(to(x, j_, z, f_))
            greet(to(x, y, j_, f_))
    loop(0, ranks, greet_owner)

    r0 = lax.broadcasted_iota(jnp.int32, (rows, rows), 0)
    r1 = lax.broadcasted_iota(jnp.int32, (rows, rows), 1)

    def flipped(r):
        p_, y_, i_ = r >> bits(run), (r >> bits(cd)) & (n - 1), r & (cd - 1)
        return (y_ * patches + p_) * cd + i_

    fetched[1].wait()
    for z_ in range(n):
        for at, part in enumerate((2, 1, 0)):
            wmine[z_, :, at * hl:(at + 1) * hl] = wq[part, :, z_ * hl:(z_ + 1) * hl]
    fetched[0].wait()
    hmine[...] = hid[...].reshape(own_rows, width)

    plain = groups - 1 + ranks - 1 + ranks + 2 * ranks

    @pl.when(z == y)
    def _():
        pl.semaphore_wait(barrier, plain - 2)

    @pl.when(z != y)
    def _():
        pl.semaphore_wait(barrier, plain)

    def send(d):
        z_ = (z + d) % n
        remote(wmine.at[z_], wbuf.at[z, x, y], WA, to(x, z_, y)).start()
    loop(1, n, send)
    pltpu.make_async_copy(wmine.at[z], wbuf.at[z, x, y], recvs.at[WA]).start()
    put_wo = pltpu.make_async_copy(wo_in, wobuf.at[x, y], fetches.at[FETCHES])
    put_wo.start()

    @pl.when(s == 0)
    def _():
        def send(z_):
            same = (z_ == z) & (z == y)

            @pl.when(same)
            def _():
                pltpu.make_async_copy(hmine, hbuf.at[y], recvs.at[HID]).start()

            @pl.when(jnp.logical_not(same))
            def _():
                remote(hmine, hbuf.at[y], HID, to(x, z_, z)).start()
        loop(0, n, send)

    class Gather:
        def __init__(self, at, block, count):
            self.at, self.block, self.count = at, block, count

        def start(self):
            for half in range(2):
                mine = self.block(half, x, y)

                def send(d, half=half, mine=mine):
                    x_, y_ = (x + d) % n, (y + d) % n
                    along_x, along_y = to(x_, z, y), to(x, z, y_)
                    near, far = (along_x, along_y) if half == 0 else (along_y, along_x)
                    mark = x if half == 0 else y
                    copy_to(mine, mine, out_first.at[self.at, half], first.at[self.at, half, mark], near).start()
                    copy_to(mine, mine, out_second.at[self.at, half], second.at[self.at, half], far).start()
                loop(1, n, send)

        def forward(self):
            for d in range(1, n):
                for half in range(2):
                    mark = ((x if half == 0 else y) + d) % n
                    part = self.block(half, mark, y) if half == 0 else self.block(half, x, mark)
                    settle(part, first.at[self.at, half, mark])

                    def send(e, half=half, part=part):
                        far = to(x, z, (y + e) % n) if half == 0 else to((x + e) % n, z, y)
                        copy_to(part, part, out_second.at[self.at, half], second.at[self.at, half], far).start()
                    loop(1, n, send)

        def wait(self):
            for half in range(2):
                settle(self.count(half, n * (n - 1)), second.at[self.at, half])

        def close(self):
            for half in range(2):
                settle(self.count(half, n - 1), out_first.at[self.at, half])
                settle(self.count(half, n * (n - 1)), out_second.at[self.at, half])

    def count_of(ref, m):
        return ref(pl.ds(0, n), pl.ds(0, n - 1)) if m == n * (n - 1) else ref(0, pl.ds(0, n - 1))

    hz = n // 2
    w_gather = Gather(
        0, lambda half, x_, y_: wbuf.at[pl.ds(half * hz, hz), x_, y_],
        lambda half, m: count_of(lambda a, b: wbuf.at[pl.ds(half * hz, hz), a, b], m))
    wide = local // 2
    o_gather = Gather(
        1, lambda half, x_, y_: wobuf.at[x_, y_, :, pl.ds(half * wide, wide)],
        lambda half, m: count_of(lambda a, b: wobuf.at[a, b, :, pl.ds(half * wide, wide)], m))
    c_gather = Gather(
        2, lambda half, x_, y_: cache.at[half, :, pl.ds(pl.multiple_of((x_ * n + y_) * run, run), run)],
        lambda half, m: cache.at[half, :, pl.ds(0, m * run)])

    arrived(wmine, WA)

    @pl.when(s == 1)
    def _():
        pl.semaphore_wait(gate, 1)
    w_gather.start()
    put_wo.wait()
    w_gather.forward()
    o_gather.start()

    for at in (2, 3, 4, 5):
        fetched[at].wait()
    length = [lens[p] for p in range(patches)]
    begin = [sum(length[:p], jnp.int32(0)) for p in range(patches)]

    def about(at, count):
        row = at + lax.broadcasted_iota(jnp.int32, (count, 1), 0)
        row_patch = row >> bits(run)
        slot = g * run + (row & (run - 1))
        return slot < pick(row_patch, length), (pick(row_patch, begin) + slot) < text[0]

    live, is_text = about(0, rows)

    def regrouped(values):
        return jnp.concatenate(
            [values[:, (x_ * n + z_) * piece:(x_ * n + z_ + 1) * piece] for z_ in range(n) for x_ in range(n)], axis=1)

    steps = mod_all.shape[1]
    chosen = (lax.broadcasted_iota(jnp.int32, (8, steps), 1) == time[0]).astype(BF16)
    for c in range(mod_all.shape[0]):
        mod[c:c + 1, :] = regrouped(matmul(chosen, mod_all[c])[0:1])

    @pl.when(s == 0)
    def _():
        arrived(hbuf, HID)
        order = (flipped(r0) == r1).astype(BF16)
        states = regrouped(matmul(order, hbuf[...].reshape(rows, width)))
        for k_ in range(ranks):
            xb[k_] = states[:, k_ * out_w:(k_ + 1) * out_w].astype(BF16)

    @pl.when(s == 1)
    def _():
        arrived(xb, X)

    step = min(16, rows)
    for at in range(0, rows, step):
        here = slice(at, at + step)
        values = jnp.concatenate([xb[k_, here, :] for k_ in range(ranks)], axis=1).astype(F32)
        mean = jnp.mean(values, axis=1, keepdims=True)
        centred = values - mean
        spread = jnp.mean(centred * centred, axis=1, keepdims=True)
        normed = centred * lax.rsqrt(spread + 1e-05)
        text_here = about(at, step)[1]
        scale = jnp.where(text_here, mod[4:5, :], mod[1:2, :])
        shift = jnp.where(text_here, mod[3:4, :], mod[0:1, :])
        mb[here, :] = (normed * (1.0 + scale) + shift).astype(BF16)

    w_gather.wait()

    @pl.when(s == 0)
    def _():
        pl.semaphore_signal(gate, 1, device_id=to(x, z, y, f, 1), device_id_type=pl.DeviceIdType.MESH)
    total = matmul(mb[...], wbuf[...].reshape(width, 3 * hl))

    head = lax.broadcasted_iota(jnp.int32, (1, hl), 1) >> bits(HEAD_DIM)

    def head_norm(values, gains):
        mean = jnp.zeros_like(values)
        for h in range(hc):
            here = head == h
            mean = jnp.where(here, jnp.sum(jnp.where(here, values, 0.0), axis=1, keepdims=True) / HEAD_DIM, mean)
        centred = values - mean
        square = centred * centred
        spread = jnp.zeros_like(values)
        for h in range(hc):
            here = head == h
            spread = jnp.where(here, jnp.sum(jnp.where(here, square, 0.0), axis=1, keepdims=True) / HEAD_DIM, spread)
        return centred * lax.rsqrt(spread + 1e-06) * jnp.concatenate([gains] * hc, axis=1)

    value_new = jnp.where(live, total[:, :hl], 0.0)
    key_new = jnp.where(live, head_norm(total[:, hl:2 * hl], gain[1:2, :]), 0.0)
    kv[g] = jnp.concatenate([value_new, key_new], axis=1).astype(BF16)

    def send(d):
        g_ = (g + d) % groups
        remote(kv.at[g], kv.at[g], KV, to(g_ // n, z, g_ % n)).start()
    loop(1, groups, send)

    def send(d):
        z_ = (z + d) % n
        remote(kv.at[g], zb.at[z], Z, to(x, z_, y)).start()
    loop(1, n, send)
    pltpu.make_async_copy(kv.at[g], zb.at[z], recvs.at[Z]).start()

    query = head_norm(total[:, 2 * hl:], gain[0:1, :])
    query = jnp.concatenate([jnp.zeros((rows, hl), F32), query], axis=1)
    lane = lax.broadcasted_iota(jnp.int32, (1, 2 * hl), 1)
    queries = jnp.concatenate(
        [jnp.where(((lane - hl) >> bits(HEAD_DIM)) == h, query, 0.0) for h in range(hc)], axis=0).astype(BF16)
    query_row = lax.broadcasted_iota(jnp.int32, (hc * rows, 1), 0)
    query_patch = (query_row & (rows - 1)) >> bits(run)
    column = lax.broadcasted_iota(jnp.int32, (1, patches * cap), 1)

    fetched[6].wait()
    for z_ in range(n):
        @pl.when(z == z_)
        def _(z_=z_):
            mine = slice(z_ * hl, (z_ + 1) * hl)
            both = jnp.concatenate([stl[1, :, :, mine], stl[0, :, :, mine]], axis=2)
            old[...] = both.reshape(patches * cap, 2 * hl)
    old_patch = column >> bits(cap)
    old_seen = ((column & (cap - 1)) < pick(old_patch, length))
    score_old = matmul_t(queries, old[...]) * HEAD_DIM ** (-0.5)
    score_old = jnp.where(old_seen & (old_patch > query_patch), score_old, HIDE)
    top_old = jnp.max(score_old, axis=1, keepdims=True)

    o_gather.forward()

    most = kv.at[pl.ds(0, groups - 1)]
    arrived(most, KV)
    new = kv[...].reshape(patches * cap, 2 * hl)
    new_patch = (column >> bits(run)) & (patches - 1)
    new_slot = (column >> bits(rows)) * run + (column & (run - 1))
    new_seen = new_slot < pick(new_patch, length)
    score_new = matmul_t(queries, new) * HEAD_DIM ** (-0.5)
    score_new = jnp.where(new_seen & (new_patch <= query_patch), score_new, HIDE)
    top = jnp.maximum(top_old, jnp.max(score_new, axis=1, keepdims=True))
    expo_old, expo_new = jnp.exp(score_old - top), jnp.exp(score_new - top)
    norm = 1.0 / (jnp.sum(expo_old, axis=1, keepdims=True) + jnp.sum(expo_new, axis=1, keepdims=True))
    taken = matmul((expo_old * norm).astype(BF16), old[...]) + matmul((expo_new * norm).astype(BF16), new)
    attended = jnp.zeros((rows, hl), F32)
    for h in range(hc):
        attended = jnp.where(head == h, taken[h * rows:(h + 1) * rows, :hl], attended)
    ab[z] = attended.astype(BF16)

    def send(d):
        remote(ab.at[z], ab.at[z], A, to(x, (z + d) % n, y)).start()
    loop(1, n, send)

    arrived(zb, Z)
    both = jnp.concatenate([zb[z_][:, hl:] for z_ in range(n)], axis=1)
    cb[0] = both.reshape(patches, run, local)
    both = jnp.concatenate([zb[z_][:, :hl] for z_ in range(n)], axis=1)
    cb[1] = both.reshape(patches, run, local)
    put = pltpu.make_async_copy(cb, cache.at[:, :, pl.ds(pl.multiple_of(g * run, run), run)], fetches.at[FETCHES + 1])
    put.start()

    o_gather.wait()
    put.wait()
    c_gather.start()
    arrived(ab.at[pl.ds(0, n - 1)], A)
    left = jnp.concatenate([ab[z_] for z_ in range(n)], axis=1)
    projected = matmul_t(left, wobuf[...].reshape(nf * out_w, local))
    for f_ in range(nf):
        osum[f_] = projected[:, f_ * out_w:(f_ + 1) * out_w]
    osend[...] = osum[1 - f].astype(BF16)
    remote(osend, orecv, F, to(x, z, y, 1 - f)).start()
    c_gather.forward()
    arrived(orecv, F)
    projected = osum[f] + orecv[...].astype(F32)
    columns = pl.ds(pl.multiple_of(k * out_w, out_w), out_w)
    gated = jnp.where(is_text, mod[5:6, columns], mod[2:3, columns])
    result = jnp.where(live, xb[k].astype(F32) + gated * projected, 0.0).astype(BF16)

    @pl.when(s == 0)
    def _():
        hbuf_x = xb.at[k]
        hbuf_x[...] = result

        def send(k_):
            remote(xb.at[k], xb.at[k], X, to(x, k_ // nf, y, k_ % nf, 1)).start()
        loop(0, ranks, send)

    back = (r0 == flipped(r1)).astype(BF16)
    ob[...] = matmul(back, result).astype(BF16).reshape(n, own_rows, out_w)

    def send(j):
        y_, f_ = j // nf, j % nf
        same = (y_ == y) & (z == y) & (f_ == f)

        @pl.when(same)
        def _():
            pltpu.make_async_copy(ob.at[y_], fin.at[k], recvs.at[FIN]).start()

        @pl.when(jnp.logical_not(same))
        def _():
            remote(ob.at[y_], fin.at[k], FIN, to(x, y, y_, f_)).start()
    loop(0, ranks, send)

    arrived(fin, FIN)
    split = out_w // piece
    natural = [fin[z_ * nf + x_ // split][:, (x_ % split) * piece:(x_ % split + 1) * piece]
               for x_ in range(n) for z_ in range(n)]
    lo[...] = jnp.concatenate(natural, axis=1).reshape(patches, cd, width)
    c_gather.wait()

    @pl.when(s == 0)
    def _():
        @pl.when(z == y)
        def _():
            sent(hbuf.at[pl.ds(0, n - 1)], HID)

        @pl.when(z != y)
        def _():
            sent(hbuf, HID)
        sent(xb, X)
    sent(wmine.at[pl.ds(0, n - 1)], WA)
    for gather in (w_gather, o_gather, c_gather):
        gather.close()
    sent(most, KV)
    sent(zb.at[pl.ds(0, n - 1)], Z)
    sent(ab.at[pl.ds(0, n - 1)], A)
    sent(osend, F)

    @pl.when(z == y)
    def _():
        sent(fin.at[pl.ds(0, ranks - 1)], FIN)

    @pl.when(z != y)
    def _():
        sent(fin, FIN)


def local(n, hidden, lengths, text_count, timestep, mod_table, w_qkv, w_out, qk_gain, stale_cache):
    nf = lax.axis_size("fsdp")
    patches, cd, width = hidden.shape
    rows_w, local_width = w_qkv.shape[1], w_qkv.shape[3]
    hl, groups, ranks = local_width // n, n * n, nf * n
    run = n * cd
    rows, out_w, own_rows, cap = patches * run, width // ranks, patches * cd, groups * run
    steps, kinds = mod_table.shape[1:3]
    vmem, anywhere = pl.BlockSpec(memory_space=pltpu.VMEM), pl.BlockSpec(memory_space=pl.ANY)
    out, cache = pl.pallas_call(
        functools.partial(relay, n, nf, patches, cd),
        out_shape=(
            jax.ShapeDtypeStruct((patches, cd, width), BF16),
            jax.ShapeDtypeStruct((2, patches, cap, local_width), BF16),
        ),
        in_specs=[anywhere] * 7 + [vmem, anywhere],
        out_specs=(vmem, anywhere),
        scratch_shapes=[
            pltpu.SMEM((patches,), jnp.int32),
            pltpu.SMEM((1,), jnp.int32),
            pltpu.SMEM((1,), jnp.int32),
            pltpu.VMEM((patches, cd, width), BF16),
            pltpu.VMEM((own_rows, width), BF16),
            pltpu.VMEM((n, own_rows, width), BF16),
            pltpu.VMEM((ranks, rows, out_w), BF16),
            pltpu.VMEM((kinds, steps, width), BF16),
            pltpu.VMEM((kinds, width), F32),
            pltpu.VMEM((rows, width), BF16),
            pltpu.VMEM((3, rows_w, local_width), BF16),
            pltpu.VMEM((n, rows_w, 3 * hl), BF16),
            pltpu.VMEM((n, n, n, rows_w, 3 * hl), BF16),
            pltpu.VMEM((n, n, rows_w, local_width), BF16),
            pltpu.VMEM((groups, rows, 2 * hl), BF16),
            pltpu.VMEM((n, rows, 2 * hl), BF16),
            pltpu.VMEM((2, patches, run, local_width), BF16),
            pltpu.VMEM((n, rows, hl), BF16),
            pltpu.VMEM((nf, rows, out_w), F32),
            pltpu.VMEM((rows, out_w), BF16),
            pltpu.VMEM((rows, out_w), BF16),
            pltpu.VMEM((n, own_rows, out_w), BF16),
            pltpu.VMEM((ranks, own_rows, out_w), BF16),
            pltpu.VMEM((2, patches, cap, local_width), BF16),
            pltpu.VMEM((patches * cap, 2 * hl), BF16),
            pltpu.SemaphoreType.DMA((FETCHES + 2,)),
            pltpu.SemaphoreType.DMA((COPIES,)),
            pltpu.SemaphoreType.DMA((COPIES,)),
            pltpu.SemaphoreType.DMA((3, 2, n)),
            pltpu.SemaphoreType.DMA((3, 2)),
            pltpu.SemaphoreType.DMA((3, 2)),
            pltpu.SemaphoreType.DMA((3, 2)),
            pltpu.SemaphoreType.REGULAR,
        ],
        compiler_params=pltpu.CompilerParams(
            collective_id=0, has_side_effects=True, vmem_limit_bytes=48 * 2**20),
    )(hidden, lengths, text_count, timestep, jnp.swapaxes(mod_table[0], 0, 1), jnp.swapaxes(w_qkv[0], 0, 1), w_out[0],
      qk_gain[0], stale_cache[0])
    return out[None], cache[None]


def solution(mesh):
    n = round(mesh.shape["tok"] ** (1 / 3))
    in_specs = (
        P(None, "tok", None),
        P(),
        P(),
        P(),
        P("section", None, None, None),
        P("section", "tok", None, "fsdp"),
        P("section", "tok", "fsdp"),
        P("section", None, None),
        P("section", None, None, None, "fsdp"),
    )
    out_specs = (P("section", None, "tok", None), P("section", None, None, None, "fsdp"))
    return jax.shard_map(
        functools.partial(local, n), mesh=mesh, in_specs=in_specs, out_specs=out_specs, check_vma=False
    )
```

```python
import functools

import jax
import jax.numpy as jnp
from jax import lax
from jax.experimental import pallas as pl
from jax.experimental.pallas import tpu as pltpu
from jax.sharding import PartitionSpec as P

HEAD_DIM = 64
F32 = jnp.float32
BF16 = jnp.bfloat16
HIDE = -1e30
HID, WA, KV, Z, A, F, X, FIN, MS, RS = range(10)
COPIES = 10
FETCHES = 7


def bits(number):
    assert number & (number - 1) == 0
    return number.bit_length() - 1


def matmul(a, b):
    return jnp.dot(a, b, preferred_element_type=F32)


def matmul_t(a, b):
    return lax.dot_general(a, b, (((1,), (1,)), ((), ())), preferred_element_type=F32)


def pick(index, values):
    out = jnp.zeros(index.shape, jnp.int32)
    for at, value in enumerate(values):
        out = jnp.where(index == at, value, out)
    return out


def relay(n, nf, patches, cd, hid_in, lens_in, text_in, time_in, mod_in, wq_in, wo_in, gain, stale, lo, cache,
          lens, text, time, hid, mine_m, all_m, mine_h, xres, xb, mod_all, mod_in_order, mod, mb, wq, wmine, wbuf, wobuf,
          part_all, part_send, part_recv, total_ref, kv, zb, cb, ab, osum, osend, orecv, ob, fin, stl, old, fetches, sends, recvs, first, second, out_first, out_second, gate):
    width = hid.shape[-1]
    rows_w = wq.shape[1]
    local = wq.shape[2]
    hl = local // n
    hc = hl // HEAD_DIM
    groups = n * n
    ranks = nf * n
    out_w = width // ranks
    run = n * cd
    rows = patches * run
    cap = groups * run
    own_rows = patches * cd
    piece = width // groups

    s, f, t = lax.axis_index("section"), lax.axis_index("fsdp"), lax.axis_index("tok")
    x, z, y = t // (n * n), (t // n) % n, t % n
    g = x * n + y
    k = z * nf + f

    def to(x_, z_, y_, f_=None, s_=None):
        return {"section": s if s_ is None else s_, "fsdp": f if f_ is None else f_, "tok": (x_ * n + z_) * n + y_}

    def copy_to(src, dst, send, recv, target):
        return pltpu.make_async_remote_copy(
            src_ref=src, dst_ref=dst, send_sem=send, recv_sem=recv, device_id=target,
            device_id_type=pl.DeviceIdType.MESH)

    def remote(src, dst, which, target):
        return copy_to(src, dst, sends.at[which], recvs.at[which], target)

    def settle(ref, sem):
        pltpu.make_async_copy(ref, ref, sem).wait()

    def sent(ref, which):
        settle(ref, sends.at[which])

    def arrived(ref, which):
        settle(ref, recvs.at[which])

    def loop(low, high, body):
        def step(i, c):
            body(i)
            return c
        lax.fori_loop(low, high, step, 0)

    fetched = [pltpu.make_async_copy(a, b, fetches.at[i]) for i, (a, b) in enumerate(
        ((hid_in, hid), (wq_in, wq), (lens_in, lens), (text_in, text), (time_in, time), (mod_in, mod_all), (stale, stl)))]
    for fetch in fetched:
        fetch.start()

    barrier = pltpu.get_barrier_semaphore()

    def greet(target):
        pl.semaphore_signal(barrier, inc=1, device_id=target, device_id_type=pl.DeviceIdType.MESH)

    def greet_plane(d):
        g_ = (g + d) % groups
        greet(to(g_ // n, z, g_ % n))
    loop(1, groups, greet_plane)

    def greet_ring(d):
        k_ = (k + d) % ranks
        greet(to(x, k_ // nf, y, k_ % nf))
    loop(1, ranks, greet_ring)

    def greet_section(k_):
        greet(to(x, k_ // nf, y, k_ % nf, 1 - s))
    loop(0, ranks, greet_section)

    def greet_planes(j):
        d, z_ = 1 + j // (n - 1), (z + 1 + j % (n - 1)) % n
        greet(to((x + d) % n, z_, y))
        greet(to(x, z_, (y + d) % n))
    loop(0, (n - 1) ** 2, greet_planes)

    r0 = lax.broadcasted_iota(jnp.int32, (rows, rows), 0)
    r1 = lax.broadcasted_iota(jnp.int32, (rows, rows), 1)

    def flipped(r):
        p_, y_, i_ = r >> bits(run), (r >> bits(cd)) & (n - 1), r & (cd - 1)
        return (y_ * patches + p_) * cd + i_

    fetched[1].wait()
    for z_ in range(n):
        for at, part in enumerate((2, 1, 0)):
            wmine[z_, :, at * hl:(at + 1) * hl] = wq[part, :, z_ * hl:(z_ + 1) * hl]

    for at in (0, 2, 3, 4, 5):
        fetched[at].wait()
    length = [lens[p] for p in range(patches)]
    begin = [sum(length[:p], jnp.int32(0)) for p in range(patches)]

    def about(first_z, count):
        row = lax.broadcasted_iota(jnp.int32, (count, 1), 0)
        row_patch = (row >> bits(cd)) & (patches - 1)
        slot = ((x * n + first_z + (row >> bits(own_rows))) * n + y) * cd + (row & (cd - 1))
        return slot < pick(row_patch, length), (pick(row_patch, begin) + slot) < text[0]

    live, is_text = about(0, rows)

    def feature(values, x_, z_):
        return values[:, (x_ * n + z_) * piece:(x_ * n + z_ + 1) * piece]

    steps = mod_all.shape[1]
    chosen = (lax.broadcasted_iota(jnp.int32, (8, steps), 1) == time[0]).astype(BF16)
    for c in range(mod_all.shape[0]):
        values = matmul(chosen, mod_all[c])[0:1]
        mod_in_order[c:c + 1, :] = values
        mod[c:c + 1, :] = jnp.concatenate([feature(values, x_, z_) for z_ in range(n) for x_ in range(n)], axis=1)

    def modulated(values, text_here, table):
        mean = jnp.mean(values, axis=1, keepdims=True)
        centred = values - mean
        spread = jnp.mean(centred * centred, axis=1, keepdims=True)
        normed = centred * lax.rsqrt(spread + 1e-05)
        scale = jnp.where(text_here, table[4:5, :], table[1:2, :])
        shift = jnp.where(text_here, table[3:4, :], table[0:1, :])
        return (normed * (1.0 + scale) + shift).astype(BF16)

    chunk = n * piece
    split = out_w // piece

    @pl.when(s == 0)
    def _():
        states = hid[...].reshape(own_rows, width)
        normed = modulated(states.astype(F32), about(z, own_rows)[1], mod_in_order)
        for x_ in range(n):
            mine_m[x_] = normed[:, x_ * chunk:(x_ + 1) * chunk]
        for f_ in range(nf):
            for z_ in range(n):
                mine_h[f_, z_] = jnp.concatenate(
                    [feature(states, f_ * split + e, z_) for e in range(split)], axis=1)

    pl.semaphore_wait(barrier, groups - 1 + ranks - 1 + ranks + 2 * (n - 1) ** 2)

    def send(d):
        z_ = (z + d) % n
        remote(wmine.at[z_], wbuf.at[z, x, y], WA, to(x, z_, y)).start()
    loop(1, n, send)
    pltpu.make_async_copy(wmine.at[z], wbuf.at[z, x, y], recvs.at[WA]).start()
    put_wo = pltpu.make_async_copy(wo_in, wobuf.at[x, y], fetches.at[FETCHES])
    put_wo.start()

    @pl.when(s == 0)
    def _():
        def send(j):
            x_, z_ = j // n, j % n
            same = (x_ == x) & (z_ == z)

            @pl.when(same)
            def _():
                pltpu.make_async_copy(mine_m.at[x], all_m.at[x * n + z], recvs.at[MS]).start()

            @pl.when(jnp.logical_not(same))
            def _():
                remote(mine_m.at[x_], all_m.at[x * n + z], MS, to(x_, z_, y)).start()
        loop(0, groups, send)

        def send(d):
            z_ = (z + d) % n
            remote(mine_h.at[f, z_], xres.at[z], HID, to(x, z_, y)).start()
        loop(1, n, send)
        pltpu.make_async_copy(mine_h.at[f, z], xres.at[z], recvs.at[HID]).start()

    class Gather:
        def __init__(self, at, block, count):
            self.at, self.block, self.count = at, block, count

        def start(self):
            for half in range(2):
                mine = self.block(half, x, y)

                def send(d, half=half, mine=mine):
                    x_, y_ = (x + d) % n, (y + d) % n
                    along_x, along_y = to(x_, z, y), to(x, z, y_)
                    near, far = (along_x, along_y) if half == 0 else (along_y, along_x)
                    mark = x if half == 0 else y
                    copy_to(mine, mine, out_first.at[self.at, half], first.at[self.at, half, mark], near).start()
                    copy_to(mine, mine, out_second.at[self.at, half], second.at[self.at, half], far).start()
                loop(1, n, send)

        def forward(self):
            for d in range(1, n):
                for half in range(2):
                    mark = ((x if half == 0 else y) + d) % n
                    part = self.block(half, mark, y) if half == 0 else self.block(half, x, mark)
                    settle(part, first.at[self.at, half, mark])

                    def send(e, half=half, part=part):
                        far = to(x, z, (y + e) % n) if half == 0 else to((x + e) % n, z, y)
                        copy_to(part, part, out_second.at[self.at, half], second.at[self.at, half], far).start()
                    loop(1, n, send)

        def wait(self):
            for half in range(2):
                settle(self.count(half, n * (n - 1)), second.at[self.at, half])

        def close(self):
            for half in range(2):
                settle(self.count(half, n - 1), out_first.at[self.at, half])
                settle(self.count(half, n * (n - 1)), out_second.at[self.at, half])

    def count_of(ref, m):
        return ref(pl.ds(0, n), pl.ds(0, n - 1)) if m == n * (n - 1) else ref(0, pl.ds(0, n - 1))

    hz = n // 2
    w_gather = Gather(
        0, lambda half, x_, y_: wbuf.at[pl.ds(half * hz, hz), x_, y_],
        lambda half, m: count_of(lambda a, b: wbuf.at[pl.ds(half * hz, hz), a, b], m))
    wide = local // 2
    o_gather = Gather(
        1, lambda half, x_, y_: wobuf.at[x_, y_, :, pl.ds(half * wide, wide)],
        lambda half, m: count_of(lambda a, b: wobuf.at[a, b, :, pl.ds(half * wide, wide)], m))
    c_gather = Gather(
        2, lambda half, x_, y_: cache.at[half, :, pl.ds(pl.multiple_of((x_ * n + y_) * run, run), run)],
        lambda half, m: cache.at[half, :, pl.ds(0, m * run)])

    arrived(wmine, WA)
    most_w = wbuf.at[:, 0, pl.ds(0, n - 1)]

    @pl.when(s == 0)
    def _():
        def send(d):
            part = wbuf.at[:, x, y]
            copy_to(part, part, out_second.at[0, 0], second.at[0, 0], to(x, z, (y + d) % n)).start()
        loop(1, n, send)
        put_wo.wait()
        o_gather.start()
        arrived(all_m, MS)
        settle(most_w, second.at[0, 0])
        pl.semaphore_signal(gate, 1, device_id=to(x, z, y, f, 1), device_id_type=pl.DeviceIdType.MESH)
        weight = wbuf[:, x].reshape(chunk, 3 * hl)
        for x_ in range(n):
            part = matmul(all_m[x_ * n:(x_ + 1) * n].reshape(rows, chunk), weight)
            part_all[x_] = part
            part_send[x_] = part.astype(BF16)

        def send(d):
            x_ = (x + d) % n
            remote(part_send.at[x_], part_recv.at[x], RS, to(x_, z, y)).start()
        loop(1, n, send)
        arrived(part_recv.at[pl.ds(0, n - 1)], RS)
        total = part_all[x]
        for d in range(1, n):
            total = total + part_recv[(x + d) % n].astype(F32)
        total_ref[...] = total

    @pl.when(s == 1)
    def _():
        pl.semaphore_wait(gate, 1)
        w_gather.start()
        put_wo.wait()
        w_gather.forward()
        o_gather.start()
        arrived(xb, X)
        for at in range(n):
            here = slice(at * own_rows, (at + 1) * own_rows)
            values = jnp.concatenate([xb[k_, here, :] for k_ in range(ranks)], axis=1).astype(F32)
            mb[here, :] = modulated(values, about(at, own_rows)[1], mod)
        w_gather.wait()
        total_ref[...] = matmul(mb[...], wbuf[...].reshape(width, 3 * hl))
    total = total_ref[...]

    head = lax.broadcasted_iota(jnp.int32, (1, hl), 1) >> bits(HEAD_DIM)

    def head_norm(values, gains):
        mean = jnp.zeros_like(values)
        for h in range(hc):
            here = head == h
            mean = jnp.where(here, jnp.sum(jnp.where(here, values, 0.0), axis=1, keepdims=True) / HEAD_DIM, mean)
        centred = values - mean
        square = centred * centred
        spread = jnp.zeros_like(values)
        for h in range(hc):
            here = head == h
            spread = jnp.where(here, jnp.sum(jnp.where(here, square, 0.0), axis=1, keepdims=True) / HEAD_DIM, spread)
        return centred * lax.rsqrt(spread + 1e-06) * jnp.concatenate([gains] * hc, axis=1)

    value_new = jnp.where(live, total[:, :hl], 0.0)
    key_new = jnp.where(live, head_norm(total[:, hl:2 * hl], gain[1:2, :]), 0.0)
    kv[g] = jnp.concatenate([value_new, key_new], axis=1).astype(BF16)

    def send(d):
        g_ = (g + d) % groups
        remote(kv.at[g], kv.at[g], KV, to(g_ // n, z, g_ % n)).start()
    loop(1, groups, send)

    def send(d):
        own_z, z_ = d // n, d % n
        part = kv.at[g, pl.ds(pl.multiple_of(own_z * own_rows, own_rows), own_rows)]
        same = (own_z == y) & (z_ == z)

        @pl.when(same)
        def _():
            pltpu.make_async_copy(part, zb.at[z * n + y], recvs.at[Z]).start()

        @pl.when(jnp.logical_not(same))
        def _():
            remote(part, zb.at[z * n + y], Z, to(x, z_, own_z)).start()
    loop(0, groups, send)

    query = head_norm(total[:, 2 * hl:], gain[0:1, :])
    query = jnp.concatenate([jnp.zeros((rows, hl), F32), query], axis=1)
    lane = lax.broadcasted_iota(jnp.int32, (1, 2 * hl), 1)
    queries = jnp.concatenate(
        [jnp.where(((lane - hl) >> bits(HEAD_DIM)) == h, query, 0.0) for h in range(hc)], axis=0).astype(BF16)
    query_row = lax.broadcasted_iota(jnp.int32, (hc * rows, 1), 0)
    query_patch = (query_row >> bits(cd)) & (patches - 1)
    column = lax.broadcasted_iota(jnp.int32, (1, patches * cap), 1)

    fetched[6].wait()
    for z_ in range(n):
        @pl.when(z == z_)
        def _(z_=z_):
            mine = slice(z_ * hl, (z_ + 1) * hl)
            both = jnp.concatenate([stl[1, :, :, mine], stl[0, :, :, mine]], axis=2)
            old[...] = both.reshape(patches * cap, 2 * hl)
    old_patch = column >> bits(cap)
    old_seen = ((column & (cap - 1)) < pick(old_patch, length))
    score_old = matmul_t(queries, old[...]) * HEAD_DIM ** (-0.5)
    score_old = jnp.where(old_seen & (old_patch > query_patch), score_old, HIDE)
    top_old = jnp.max(score_old, axis=1, keepdims=True)

    o_gather.forward()

    most = kv.at[pl.ds(0, groups - 1)]
    arrived(most, KV)
    new = kv[...].reshape(patches * cap, 2 * hl)
    new_patch = (column >> bits(cd)) & (patches - 1)
    new_group, new_z = column >> bits(rows), (column >> bits(own_rows)) & (n - 1)
    new_tok = ((new_group >> bits(n)) * n + new_z) * n + (new_group & (n - 1))
    new_slot = new_tok * cd + (column & (cd - 1))
    new_seen = new_slot < pick(new_patch, length)
    score_new = matmul_t(queries, new) * HEAD_DIM ** (-0.5)
    score_new = jnp.where(new_seen & (new_patch <= query_patch), score_new, HIDE)
    top = jnp.maximum(top_old, jnp.max(score_new, axis=1, keepdims=True))
    expo_old, expo_new = jnp.exp(score_old - top), jnp.exp(score_new - top)
    norm = 1.0 / (jnp.sum(expo_old, axis=1, keepdims=True) + jnp.sum(expo_new, axis=1, keepdims=True))
    taken = matmul((expo_old * norm).astype(BF16), old[...]) + matmul((expo_new * norm).astype(BF16), new)
    attended = jnp.zeros((rows, hl), F32)
    for h in range(hc):
        attended = jnp.where(head == h, taken[h * rows:(h + 1) * rows, :hl], attended)
    ab[z] = attended.astype(BF16)

    def send(d):
        remote(ab.at[z], ab.at[z], A, to(x, (z + d) % n, y)).start()
    loop(1, n, send)

    arrived(zb, Z)
    order = (flipped(r0) == r1).astype(BF16)
    for at, lanes in enumerate((slice(hl, 2 * hl), slice(0, hl))):
        both = jnp.concatenate([zb[z_ * n:(z_ + 1) * n].reshape(rows, 2 * hl)[:, lanes] for z_ in range(n)], axis=1)
        cb[at] = matmul(order, both).astype(BF16).reshape(patches, run, local)
    put = pltpu.make_async_copy(cb, cache.at[:, :, pl.ds(pl.multiple_of(g * run, run), run)], fetches.at[FETCHES + 1])
    put.start()

    o_gather.wait()
    put.wait()
    c_gather.start()
    arrived(ab.at[pl.ds(0, n - 1)], A)
    left = jnp.concatenate([ab[z_] for z_ in range(n)], axis=1)
    projected = matmul_t(left, wobuf[...].reshape(nf * out_w, local))
    for f_ in range(nf):
        osum[f_] = projected[:, f_ * out_w:(f_ + 1) * out_w]
    osend[...] = osum[1 - f].astype(BF16)
    remote(osend, orecv, F, to(x, z, y, 1 - f)).start()
    c_gather.forward()
    arrived(orecv, F)
    projected = osum[f] + orecv[...].astype(F32)
    columns = pl.ds(pl.multiple_of(k * out_w, out_w), out_w)
    gated = jnp.where(is_text, mod[5:6, columns], mod[2:3, columns])

    @pl.when(s == 0)
    def _():
        arrived(xres, HID)
        xb[k] = xres[...].reshape(rows, out_w)
    result = jnp.where(live, xb[k].astype(F32) + gated * projected, 0.0).astype(BF16)
    ob[...] = result

    @pl.when(s == 0)
    def _():
        def send(k_):
            remote(ob, xb.at[k], X, to(x, k_ // nf, y, k_ % nf, 1)).start()
        loop(0, ranks, send)

    def own(z_):
        return ob.at[pl.ds(pl.multiple_of(z_ * own_rows, own_rows), own_rows)]

    def send(d):
        k_ = (k + d) % ranks
        remote(own(k_ // nf), fin.at[k], FIN, to(x, k_ // nf, y, k_ % nf)).start()
    loop(1, ranks, send)
    pltpu.make_async_copy(own(z), fin.at[k], recvs.at[FIN]).start()

    arrived(fin, FIN)
    natural = [fin[z_ * nf + x_ // split][:, (x_ % split) * piece:(x_ % split + 1) * piece]
               for x_ in range(n) for z_ in range(n)]
    lo[...] = jnp.concatenate(natural, axis=1).reshape(patches, cd, width)
    c_gather.wait()

    sent(wmine.at[pl.ds(0, n - 1)], WA)

    @pl.when(s == 0)
    def _():
        sent(all_m.at[0:groups - 1], MS)
        sent(xres.at[pl.ds(0, n - 1)], HID)
        settle(most_w, out_second.at[0, 0])
        sent(part_send.at[pl.ds(0, n - 1)], RS)
        sent(xb, X)

    @pl.when(s == 1)
    def _():
        w_gather.close()
    o_gather.close()
    c_gather.close()
    sent(most, KV)
    sent(zb.at[0:groups - 1], Z)
    sent(ab.at[pl.ds(0, n - 1)], A)
    sent(osend, F)

    sent(fin.at[pl.ds(0, ranks - 1)], FIN)


def local(n, hidden, lengths, text_count, timestep, mod_table, w_qkv, w_out, qk_gain, stale_cache):
    nf = lax.axis_size("fsdp")
    patches, cd, width = hidden.shape
    rows_w, local_width = w_qkv.shape[1], w_qkv.shape[3]
    hl, groups, ranks = local_width // n, n * n, nf * n
    run = n * cd
    rows, out_w, own_rows, cap = patches * run, width // ranks, patches * cd, groups * run
    steps, kinds = mod_table.shape[1:3]
    vmem, anywhere = pl.BlockSpec(memory_space=pltpu.VMEM), pl.BlockSpec(memory_space=pl.ANY)
    out, cache = pl.pallas_call(
        functools.partial(relay, n, nf, patches, cd),
        out_shape=(
            jax.ShapeDtypeStruct((patches, cd, width), BF16),
            jax.ShapeDtypeStruct((2, patches, cap, local_width), BF16),
        ),
        in_specs=[anywhere] * 7 + [vmem, anywhere],
        out_specs=(vmem, anywhere),
        scratch_shapes=[
            pltpu.SMEM((patches,), jnp.int32),
            pltpu.SMEM((1,), jnp.int32),
            pltpu.SMEM((1,), jnp.int32),
            pltpu.VMEM((patches, cd, width), BF16),
            pltpu.VMEM((n, own_rows, width // n), BF16),
            pltpu.VMEM((groups, own_rows, width // n), BF16),
            pltpu.VMEM((nf, n, own_rows, out_w), BF16),
            pltpu.VMEM((n, own_rows, out_w), BF16),
            pltpu.VMEM((ranks, rows, out_w), BF16),
            pltpu.VMEM((kinds, steps, width), BF16),
            pltpu.VMEM((kinds, width), F32),
            pltpu.VMEM((kinds, width), F32),
            pltpu.VMEM((rows, width), BF16),
            pltpu.VMEM((3, rows_w, local_width), BF16),
            pltpu.VMEM((n, rows_w, 3 * hl), BF16),
            pltpu.VMEM((n, n, n, rows_w, 3 * hl), BF16),
            pltpu.VMEM((n, n, rows_w, local_width), BF16),
            pltpu.VMEM((n, rows, 3 * hl), F32),
            pltpu.VMEM((n, rows, 3 * hl), BF16),
            pltpu.VMEM((n, rows, 3 * hl), BF16),
            pltpu.VMEM((rows, 3 * hl), F32),
            pltpu.VMEM((groups, rows, 2 * hl), BF16),
            pltpu.VMEM((groups, own_rows, 2 * hl), BF16),
            pltpu.VMEM((2, patches, run, local_width), BF16),
            pltpu.VMEM((n, rows, hl), BF16),
            pltpu.VMEM((nf, rows, out_w), F32),
            pltpu.VMEM((rows, out_w), BF16),
            pltpu.VMEM((rows, out_w), BF16),
            pltpu.VMEM((rows, out_w), BF16),
            pltpu.VMEM((ranks, own_rows, out_w), BF16),
            pltpu.VMEM((2, patches, cap, local_width), BF16),
            pltpu.VMEM((patches * cap, 2 * hl), BF16),
            pltpu.SemaphoreType.DMA((FETCHES + 2,)),
            pltpu.SemaphoreType.DMA((COPIES,)),
            pltpu.SemaphoreType.DMA((COPIES,)),
            pltpu.SemaphoreType.DMA((3, 2, n)),
            pltpu.SemaphoreType.DMA((3, 2)),
            pltpu.SemaphoreType.DMA((3, 2)),
            pltpu.SemaphoreType.DMA((3, 2)),
            pltpu.SemaphoreType.REGULAR,
        ],
        compiler_params=pltpu.CompilerParams(
            collective_id=0, has_side_effects=True, vmem_limit_bytes=62 * 2**20),
    )(hidden, lengths, text_count, timestep, jnp.swapaxes(mod_table[0], 0, 1), jnp.swapaxes(w_qkv[0], 0, 1), w_out[0],
      qk_gain[0], stale_cache[0])
    return out[None], cache[None]


def solution(mesh):
    n = round(mesh.shape["tok"] ** (1 / 3))
    in_specs = (
        P(None, "tok", None),
        P(),
        P(),
        P(),
        P("section", None, None, None),
        P("section", "tok", None, "fsdp"),
        P("section", "tok", "fsdp"),
        P("section", None, None),
        P("section", None, None, None, "fsdp"),
    )
    out_specs = (P("section", None, "tok", None), P("section", None, None, None, "fsdp"))
    return jax.shard_map(
        functools.partial(local, n), mesh=mesh, in_specs=in_specs, out_specs=out_specs, check_vma=False
    )
```

```python
import functools

import jax
import jax.numpy as jnp
from jax import lax
from jax.experimental import pallas as pl
from jax.experimental.pallas import tpu as pltpu
from jax.sharding import PartitionSpec as P

HEAD_DIM = 64
F32 = jnp.float32
BF16 = jnp.bfloat16
HIDE = -1e30
HID, WA, Z, A, F, X, FIN, MS, RS = range(9)
COPIES = 9
FETCHES = 7


def bits(number):
    assert number & (number - 1) == 0
    return number.bit_length() - 1


def matmul(a, b):
    return jnp.dot(a, b, preferred_element_type=F32)


def matmul_t(a, b):
    return lax.dot_general(a, b, (((1,), (1,)), ((), ())), preferred_element_type=F32)


def pick(index, values):
    out = jnp.zeros(index.shape, jnp.int32)
    for at, value in enumerate(values):
        out = jnp.where(index == at, value, out)
    return out


def relay(n, nf, patches, cd, hid_in, lens_in, text_in, time_in, mod_in, wq_in, wo_in, gain, stale, lo, cache,
          lens, text, time, hid, mine_m, all_m, mine_h, xres, xb, mod_all, mod_in_order, mod, mb, wq, wmine, wbuf, wobuf,
          part_all, part_send, part_recv, total_ref, kv, zb, ab, osum, osend, orecv, ob, fin, cv, stl, old, fetches, sends, recvs, first, second, out_first, out_second, put_sems, gate):
    width = hid.shape[-1]
    rows_w = wq.shape[1]
    local = wq.shape[2]
    hl = local // n
    hc = hl // HEAD_DIM
    groups = n * n
    ranks = nf * n
    out_w = width // ranks
    run = n * cd
    rows = patches * run
    cap = groups * run
    own_rows = patches * cd
    piece = width // groups

    s, f, t = lax.axis_index("section"), lax.axis_index("fsdp"), lax.axis_index("tok")
    x, z, y = t // (n * n), (t // n) % n, t % n
    g = x * n + y
    k = z * nf + f

    def to(x_, z_, y_, f_=None, s_=None):
        return {"section": s if s_ is None else s_, "fsdp": f if f_ is None else f_, "tok": (x_ * n + z_) * n + y_}

    def copy_to(src, dst, send, recv, target):
        return pltpu.make_async_remote_copy(
            src_ref=src, dst_ref=dst, send_sem=send, recv_sem=recv, device_id=target,
            device_id_type=pl.DeviceIdType.MESH)

    def remote(src, dst, which, target):
        return copy_to(src, dst, sends.at[which], recvs.at[which], target)

    def settle(ref, sem):
        pltpu.make_async_copy(ref, ref, sem).wait()

    def sent(ref, which):
        settle(ref, sends.at[which])

    def arrived(ref, which):
        settle(ref, recvs.at[which])

    def loop(low, high, body):
        def step(i, c):
            body(i)
            return c
        lax.fori_loop(low, high, step, 0)

    fetched = [pltpu.make_async_copy(a, b, fetches.at[i]) for i, (a, b) in enumerate(
        ((hid_in, hid), (wq_in, wq), (lens_in, lens), (text_in, text), (time_in, time), (mod_in, mod_all), (stale, stl)))]
    for fetch in fetched:
        fetch.start()

    barrier = pltpu.get_barrier_semaphore()

    def greet(target):
        pl.semaphore_signal(barrier, inc=1, device_id=target, device_id_type=pl.DeviceIdType.MESH)

    def greet_plane(d):
        g_ = (g + d) % groups
        greet(to(g_ // n, z, g_ % n))
    loop(1, groups, greet_plane)

    def greet_ring(d):
        k_ = (k + d) % ranks
        greet(to(x, k_ // nf, y, k_ % nf))
    loop(1, ranks, greet_ring)

    def greet_section(k_):
        greet(to(x, k_ // nf, y, k_ % nf, 1 - s))
    loop(0, ranks, greet_section)

    def greet_planes(j):
        d, z_ = 1 + j // (n - 1), (z + 1 + j % (n - 1)) % n
        greet(to((x + d) % n, z_, y))
        greet(to(x, z_, (y + d) % n))
    loop(0, (n - 1) ** 2, greet_planes)

    r0 = lax.broadcasted_iota(jnp.int32, (rows, rows), 0)
    r1 = lax.broadcasted_iota(jnp.int32, (rows, rows), 1)

    def flipped(r):
        p_, y_, i_ = r >> bits(run), (r >> bits(cd)) & (n - 1), r & (cd - 1)
        return (y_ * patches + p_) * cd + i_

    fetched[1].wait()
    for z_ in range(n):
        for at, part in enumerate((2, 1, 0)):
            wmine[z_, :, at * hl:(at + 1) * hl] = wq[part, :, z_ * hl:(z_ + 1) * hl]

    for at in (0, 2, 3, 4, 5):
        fetched[at].wait()
    length = [lens[p] for p in range(patches)]
    begin = [sum(length[:p], jnp.int32(0)) for p in range(patches)]

    def about(first_z, count):
        row = lax.broadcasted_iota(jnp.int32, (count, 1), 0)
        row_patch = (row >> bits(cd)) & (patches - 1)
        slot = ((x * n + first_z + (row >> bits(own_rows))) * n + y) * cd + (row & (cd - 1))
        return slot < pick(row_patch, length), (pick(row_patch, begin) + slot) < text[0]

    live, is_text = about(0, rows)

    def feature(values, x_, z_):
        return values[:, (x_ * n + z_) * piece:(x_ * n + z_ + 1) * piece]

    steps = mod_all.shape[1]
    chosen = (lax.broadcasted_iota(jnp.int32, (8, steps), 1) == time[0]).astype(BF16)
    for c in range(mod_all.shape[0]):
        values = matmul(chosen, mod_all[c])[0:1]
        mod_in_order[c:c + 1, :] = values
        mod[c:c + 1, :] = jnp.concatenate([feature(values, x_, z_) for z_ in range(n) for x_ in range(n)], axis=1)

    def modulated(values, text_here, table):
        mean = jnp.mean(values, axis=1, keepdims=True)
        centred = values - mean
        spread = jnp.mean(centred * centred, axis=1, keepdims=True)
        normed = centred * lax.rsqrt(spread + 1e-05)
        scale = jnp.where(text_here, table[4:5, :], table[1:2, :])
        shift = jnp.where(text_here, table[3:4, :], table[0:1, :])
        return (normed * (1.0 + scale) + shift).astype(BF16)

    chunk = n * piece
    split = out_w // piece

    @pl.when(s == 0)
    def _():
        states = hid[...].reshape(own_rows, width)
        normed = modulated(states.astype(F32), about(z, own_rows)[1], mod_in_order)
        for x_ in range(n):
            mine_m[x_] = normed[:, x_ * chunk:(x_ + 1) * chunk]
        for f_ in range(nf):
            for z_ in range(n):
                mine_h[f_, z_] = jnp.concatenate(
                    [feature(states, f_ * split + e, z_) for e in range(split)], axis=1)

    pl.semaphore_wait(barrier, groups - 1 + ranks - 1 + ranks + 2 * (n - 1) ** 2)

    def send(d):
        z_ = (z + d) % n
        remote(wmine.at[z_], wbuf.at[z, x, y], WA, to(x, z_, y)).start()
    loop(1, n, send)
    pltpu.make_async_copy(wmine.at[z], wbuf.at[z, x, y], recvs.at[WA]).start()
    put_wo = pltpu.make_async_copy(wo_in, wobuf.at[x, y], fetches.at[FETCHES])
    put_wo.start()

    @pl.when(s == 0)
    def _():
        def send(j):
            x_, z_ = j // n, j % n
            same = (x_ == x) & (z_ == z)

            @pl.when(same)
            def _():
                pltpu.make_async_copy(mine_m.at[x], all_m.at[x * n + z], recvs.at[MS]).start()

            @pl.when(jnp.logical_not(same))
            def _():
                remote(mine_m.at[x_], all_m.at[x * n + z], MS, to(x_, z_, y)).start()
        loop(0, groups, send)

        def send(d):
            z_ = (z + d) % n
            remote(mine_h.at[f, z_], xres.at[z], HID, to(x, z_, y)).start()
        loop(1, n, send)
        pltpu.make_async_copy(mine_h.at[f, z], xres.at[z], recvs.at[HID]).start()

    class Gather:
        def __init__(self, at, block, count):
            self.at, self.block, self.count = at, block, count

        def start(self):
            for half in range(2):
                mine = self.block(half, x, y)

                def send(d, half=half, mine=mine):
                    x_, y_ = (x + d) % n, (y + d) % n
                    along_x, along_y = to(x_, z, y), to(x, z, y_)
                    near, far = (along_x, along_y) if half == 0 else (along_y, along_x)
                    mark = x if half == 0 else y
                    copy_to(mine, mine, out_first.at[self.at, half], first.at[self.at, half, mark], near).start()
                    copy_to(mine, mine, out_second.at[self.at, half], second.at[self.at, half], far).start()
                loop(1, n, send)

        def forward(self):
            for d in range(1, n):
                for half in range(2):
                    mark = ((x if half == 0 else y) + d) % n
                    part = self.block(half, mark, y) if half == 0 else self.block(half, x, mark)
                    settle(part, first.at[self.at, half, mark])

                    def send(e, half=half, part=part):
                        far = to(x, z, (y + e) % n) if half == 0 else to((x + e) % n, z, y)
                        copy_to(part, part, out_second.at[self.at, half], second.at[self.at, half], far).start()
                    loop(1, n, send)

        def wait(self):
            for half in range(2):
                settle(self.count(half, n * (n - 1)), second.at[self.at, half])

        def close(self):
            for half in range(2):
                settle(self.count(half, n - 1), out_first.at[self.at, half])
                settle(self.count(half, n * (n - 1)), out_second.at[self.at, half])

    def count_of(ref, m):
        return ref(pl.ds(0, n), pl.ds(0, n - 1)) if m == n * (n - 1) else ref(0, pl.ds(0, n - 1))

    hz = n // 2
    w_gather = Gather(
        0, lambda half, x_, y_: wbuf.at[pl.ds(half * hz, hz), x_, y_],
        lambda half, m: count_of(lambda a, b: wbuf.at[pl.ds(half * hz, hz), a, b], m))
    wide = local // 2
    o_gather = Gather(
        1, lambda half, x_, y_: wobuf.at[x_, y_, :, pl.ds(half * wide, wide)],
        lambda half, m: count_of(lambda a, b: wobuf.at[a, b, :, pl.ds(half * wide, wide)], m))
    hr = rows // 2
    kv_gather = Gather(
        3, lambda half, x_, y_: kv.at[x_ * n + y_, pl.ds(half * hr, hr)],
        lambda half, m: kv.at[pl.ds(0, m), pl.ds(half * hr, hr)])
    c_gather = Gather(
        2, lambda half, x_, y_: cv.at[half, :, pl.ds(pl.multiple_of((x_ * n + y_) * run, run), run)],
        lambda half, m: cv.at[half, :, pl.ds(0, m * run)])

    arrived(wmine, WA)
    most_w = wbuf.at[:, 0, pl.ds(0, n - 1)]

    @pl.when(s == 0)
    def _():
        def send(d):
            part = wbuf.at[:, x, y]
            copy_to(part, part, out_second.at[0, 0], second.at[0, 0], to(x, z, (y + d) % n)).start()
        loop(1, n, send)
        put_wo.wait()
        o_gather.start()
        arrived(all_m, MS)
        settle(most_w, second.at[0, 0])
        pl.semaphore_signal(gate, 1, device_id=to(x, z, y, f, 1), device_id_type=pl.DeviceIdType.MESH)
        weight = wbuf[:, x].reshape(chunk, 3 * hl)
        for x_ in range(n):
            part = matmul(all_m[x_ * n:(x_ + 1) * n].reshape(rows, chunk), weight)
            part_all[x_] = part
            part_send[x_] = part.astype(BF16)

        def send(d):
            x_ = (x + d) % n
            remote(part_send.at[x_], part_recv.at[x], RS, to(x_, z, y)).start()
        loop(1, n, send)
        arrived(part_recv.at[pl.ds(0, n - 1)], RS)
        total = part_all[x]
        for d in range(1, n):
            total = total + part_recv[(x + d) % n].astype(F32)
        total_ref[...] = total

    @pl.when(s == 1)
    def _():
        pl.semaphore_wait(gate, 1)
        w_gather.start()
        put_wo.wait()
        w_gather.forward()
        o_gather.start()
        arrived(xb, X)
        for at in range(n):
            here = slice(at * own_rows, (at + 1) * own_rows)
            values = jnp.concatenate([xb[k_, here, :] for k_ in range(ranks)], axis=1).astype(F32)
            mb[here, :] = modulated(values, about(at, own_rows)[1], mod)
        w_gather.wait()
        total_ref[...] = matmul(mb[...], wbuf[...].reshape(width, 3 * hl))
    total = total_ref[...]

    head = lax.broadcasted_iota(jnp.int32, (1, hl), 1) >> bits(HEAD_DIM)

    def head_norm(values, gains):
        mean = jnp.zeros_like(values)
        for h in range(hc):
            here = head == h
            mean = jnp.where(here, jnp.sum(jnp.where(here, values, 0.0), axis=1, keepdims=True) / HEAD_DIM, mean)
        centred = values - mean
        square = centred * centred
        spread = jnp.zeros_like(values)
        for h in range(hc):
            here = head == h
            spread = jnp.where(here, jnp.sum(jnp.where(here, square, 0.0), axis=1, keepdims=True) / HEAD_DIM, spread)
        return centred * lax.rsqrt(spread + 1e-06) * jnp.concatenate([gains] * hc, axis=1)

    value_new = jnp.where(live, total[:, :hl], 0.0)
    key_new = jnp.where(live, head_norm(total[:, hl:2 * hl], gain[1:2, :]), 0.0)
    kv[g] = jnp.concatenate([value_new, key_new], axis=1).astype(BF16)

    kv_gather.start()

    def send(d):
        own_z, z_ = d // n, d % n
        part = kv.at[g, pl.ds(pl.multiple_of(own_z * own_rows, own_rows), own_rows)]
        same = (own_z == y) & (z_ == z)

        @pl.when(same)
        def _():
            pltpu.make_async_copy(part, zb.at[z * n + y], recvs.at[Z]).start()

        @pl.when(jnp.logical_not(same))
        def _():
            remote(part, zb.at[z * n + y], Z, to(x, z_, own_z)).start()
    loop(0, groups, send)

    query = head_norm(total[:, 2 * hl:], gain[0:1, :])
    query = jnp.concatenate([jnp.zeros((rows, hl), F32), query], axis=1)
    lane = lax.broadcasted_iota(jnp.int32, (1, 2 * hl), 1)
    queries = jnp.concatenate(
        [jnp.where(((lane - hl) >> bits(HEAD_DIM)) == h, query, 0.0) for h in range(hc)], axis=0).astype(BF16)
    query_row = lax.broadcasted_iota(jnp.int32, (hc * rows, 1), 0)
    query_patch = (query_row >> bits(cd)) & (patches - 1)
    column = lax.broadcasted_iota(jnp.int32, (1, patches * cap), 1)

    fetched[6].wait()
    for z_ in range(n):
        @pl.when(z == z_)
        def _(z_=z_):
            mine = slice(z_ * hl, (z_ + 1) * hl)
            both = jnp.concatenate([stl[1, :, :, mine], stl[0, :, :, mine]], axis=2)
            old[...] = both.reshape(patches * cap, 2 * hl)
    old_patch = column >> bits(cap)
    old_seen = ((column & (cap - 1)) < pick(old_patch, length))
    kv_gather.forward()
    score_old = matmul_t(queries, old[...]) * HEAD_DIM ** (-0.5)
    score_old = jnp.where(old_seen & (old_patch > query_patch), score_old, HIDE)
    top_old = jnp.max(score_old, axis=1, keepdims=True)

    o_gather.forward()

    kv_gather.wait()
    new = kv[...].reshape(patches * cap, 2 * hl)
    new_patch = (column >> bits(cd)) & (patches - 1)
    new_group, new_z = column >> bits(rows), (column >> bits(own_rows)) & (n - 1)
    new_tok = ((new_group >> bits(n)) * n + new_z) * n + (new_group & (n - 1))
    new_slot = new_tok * cd + (column & (cd - 1))
    new_seen = new_slot < pick(new_patch, length)
    score_new = matmul_t(queries, new) * HEAD_DIM ** (-0.5)
    score_new = jnp.where(new_seen & (new_patch <= query_patch), score_new, HIDE)
    top = jnp.maximum(top_old, jnp.max(score_new, axis=1, keepdims=True))
    expo_old, expo_new = jnp.exp(score_old - top), jnp.exp(score_new - top)
    norm = 1.0 / (jnp.sum(expo_old, axis=1, keepdims=True) + jnp.sum(expo_new, axis=1, keepdims=True))
    taken = matmul((expo_old * norm).astype(BF16), old[...]) + matmul((expo_new * norm).astype(BF16), new)
    attended = jnp.zeros((rows, hl), F32)
    for h in range(hc):
        attended = jnp.where(head == h, taken[h * rows:(h + 1) * rows, :hl], attended)
    ab[z] = attended.astype(BF16)

    def send(d):
        remote(ab.at[z], ab.at[z], A, to(x, (z + d) % n, y)).start()
    loop(1, n, send)

    arrived(zb, Z)
    order = (flipped(r0) == r1).astype(BF16)
    for at, lanes in enumerate((slice(hl, 2 * hl), slice(0, hl))):
        both = jnp.concatenate([zb[z_ * n:(z_ + 1) * n].reshape(rows, 2 * hl)[:, lanes] for z_ in range(n)], axis=1)
        cv[at, :, pl.ds(pl.multiple_of(g * run, run), run), :] = matmul(order, both).astype(BF16).reshape(patches, run, local)

    o_gather.wait()
    c_gather.start()
    arrived(ab.at[pl.ds(0, n - 1)], A)
    left = jnp.concatenate([ab[z_] for z_ in range(n)], axis=1)
    projected = matmul_t(left, wobuf[...].reshape(nf * out_w, local))
    for f_ in range(nf):
        osum[f_] = projected[:, f_ * out_w:(f_ + 1) * out_w]
    osend[...] = osum[1 - f].astype(BF16)
    remote(osend, orecv, F, to(x, z, y, 1 - f)).start()
    c_gather.forward()
    arrived(orecv, F)
    projected = osum[f] + orecv[...].astype(F32)
    columns = pl.ds(pl.multiple_of(k * out_w, out_w), out_w)
    gated = jnp.where(is_text, mod[5:6, columns], mod[2:3, columns])

    @pl.when(s == 0)
    def _():
        arrived(xres, HID)
        xb[k] = xres[...].reshape(rows, out_w)
    result = jnp.where(live, xb[k].astype(F32) + gated * projected, 0.0).astype(BF16)
    ob[...] = result

    @pl.when(s == 0)
    def _():
        def send(k_):
            remote(ob, xb.at[k], X, to(x, k_ // nf, y, k_ % nf, 1)).start()
        loop(0, ranks, send)

    def own(z_):
        return ob.at[pl.ds(pl.multiple_of(z_ * own_rows, own_rows), own_rows)]

    def send(d):
        k_ = (k + d) % ranks
        remote(own(k_ // nf), fin.at[k], FIN, to(x, k_ // nf, y, k_ % nf)).start()
    loop(1, ranks, send)
    pltpu.make_async_copy(own(z), fin.at[k], recvs.at[FIN]).start()

    arrived(fin, FIN)
    natural = [fin[z_ * nf + x_ // split][:, (x_ % split) * piece:(x_ % split + 1) * piece]
               for x_ in range(n) for z_ in range(n)]
    lo[...] = jnp.concatenate(natural, axis=1).reshape(patches, cd, width)
    c_gather.wait()
    puts = [pltpu.make_async_copy(cv.at[c, p], cache.at[c, p], put_sems.at[c, p]) for c in range(2) for p in range(patches)]
    for put in puts:
        put.start()

    sent(wmine.at[pl.ds(0, n - 1)], WA)

    @pl.when(s == 0)
    def _():
        sent(all_m.at[0:groups - 1], MS)
        sent(xres.at[pl.ds(0, n - 1)], HID)
        settle(most_w, out_second.at[0, 0])
        sent(part_send.at[pl.ds(0, n - 1)], RS)
        sent(xb, X)

    @pl.when(s == 1)
    def _():
        w_gather.close()
    o_gather.close()
    c_gather.close()
    kv_gather.close()
    sent(zb.at[0:groups - 1], Z)
    sent(ab.at[pl.ds(0, n - 1)], A)
    sent(osend, F)

    sent(fin.at[pl.ds(0, ranks - 1)], FIN)
    for put in puts:
        put.wait()


def hand_back(out, cache, lo, new_cache, out_v, cache_v, sems):
    parts = [(out, out_v, lo)]
    for c in range(cache.shape[0]):
        for p in range(cache.shape[1]):
            parts.append((cache.at[c, p], cache_v.at[c, p], new_cache.at[c, p]))
    fetches = [pltpu.make_async_copy(a, b, sems.at[0, i]) for i, (a, b, _) in enumerate(parts)]
    puts = [pltpu.make_async_copy(b, c, sems.at[1, i]) for i, (_, b, c) in enumerate(parts)]
    for fetch in fetches:
        fetch.start()
    for fetch, put in zip(fetches, puts):
        fetch.wait()
        put.start()
    for put in puts:
        put.wait()


def local(n, hidden, lengths, text_count, timestep, mod_table, w_qkv, w_out, qk_gain, stale_cache):
    nf = lax.axis_size("fsdp")
    patches, cd, width = hidden.shape
    rows_w, local_width = w_qkv.shape[1], w_qkv.shape[3]
    hl, groups, ranks = local_width // n, n * n, nf * n
    run = n * cd
    rows, out_w, own_rows, cap = patches * run, width // ranks, patches * cd, groups * run
    steps, kinds = mod_table.shape[1:3]
    vmem, anywhere = pl.BlockSpec(memory_space=pltpu.VMEM), pl.BlockSpec(memory_space=pl.ANY)
    out, cache = pl.pallas_call(
        functools.partial(relay, n, nf, patches, cd),
        out_shape=(
            jax.ShapeDtypeStruct((patches, cd, width), BF16),
            jax.ShapeDtypeStruct((2, patches, cap, local_width), BF16),
        ),
        in_specs=[anywhere] * 7 + [vmem, anywhere],
        out_specs=(vmem, anywhere),
        scratch_shapes=[
            pltpu.SMEM((patches,), jnp.int32),
            pltpu.SMEM((1,), jnp.int32),
            pltpu.SMEM((1,), jnp.int32),
            pltpu.VMEM((patches, cd, width), BF16),
            pltpu.VMEM((n, own_rows, width // n), BF16),
            pltpu.VMEM((groups, own_rows, width // n), BF16),
            pltpu.VMEM((nf, n, own_rows, out_w), BF16),
            pltpu.VMEM((n, own_rows, out_w), BF16),
            pltpu.VMEM((ranks, rows, out_w), BF16),
            pltpu.VMEM((kinds, steps, width), BF16),
            pltpu.VMEM((kinds, width), F32),
            pltpu.VMEM((kinds, width), F32),
            pltpu.VMEM((rows, width), BF16),
            pltpu.VMEM((3, rows_w, local_width), BF16),
            pltpu.VMEM((n, rows_w, 3 * hl), BF16),
            pltpu.VMEM((n, n, n, rows_w, 3 * hl), BF16),
            pltpu.VMEM((n, n, rows_w, local_width), BF16),
            pltpu.VMEM((n, rows, 3 * hl), F32),
            pltpu.VMEM((n, rows, 3 * hl), BF16),
            pltpu.VMEM((n, rows, 3 * hl), BF16),
            pltpu.VMEM((rows, 3 * hl), F32),
            pltpu.VMEM((groups, rows, 2 * hl), BF16),
            pltpu.VMEM((groups, own_rows, 2 * hl), BF16),
            pltpu.VMEM((n, rows, hl), BF16),
            pltpu.VMEM((nf, rows, out_w), F32),
            pltpu.VMEM((rows, out_w), BF16),
            pltpu.VMEM((rows, out_w), BF16),
            pltpu.VMEM((rows, out_w), BF16),
            pltpu.VMEM((ranks, own_rows, out_w), BF16),
            pltpu.VMEM((2, patches, cap, local_width), BF16),
            pltpu.VMEM((2, patches, cap, local_width), BF16),
            pltpu.VMEM((patches * cap, 2 * hl), BF16),
            pltpu.SemaphoreType.DMA((FETCHES + 1,)),
            pltpu.SemaphoreType.DMA((COPIES,)),
            pltpu.SemaphoreType.DMA((COPIES,)),
            pltpu.SemaphoreType.DMA((4, 2, n)),
            pltpu.SemaphoreType.DMA((4, 2)),
            pltpu.SemaphoreType.DMA((4, 2)),
            pltpu.SemaphoreType.DMA((4, 2)),
            pltpu.SemaphoreType.DMA((2, patches)),
            pltpu.SemaphoreType.REGULAR,
        ],
        compiler_params=pltpu.CompilerParams(
            collective_id=0, has_side_effects=True, vmem_limit_bytes=62 * 2**20),
    )(hidden, lengths, text_count, timestep, jnp.swapaxes(mod_table[0], 0, 1), jnp.swapaxes(w_qkv[0], 0, 1), w_out[0],
      qk_gain[0], stale_cache[0])
    out, cache = pl.pallas_call(
        hand_back,
        out_shape=(jax.ShapeDtypeStruct(out.shape, BF16), jax.ShapeDtypeStruct(cache.shape, BF16)),
        in_specs=[anywhere] * 2,
        out_specs=(anywhere, anywhere),
        scratch_shapes=[
            pltpu.VMEM(out.shape, BF16),
            pltpu.VMEM(cache.shape, BF16),
            pltpu.SemaphoreType.DMA((2, 1 + 2 * patches)),
        ],
        compiler_params=pltpu.CompilerParams(vmem_limit_bytes=62 * 2**20),
    )(out, cache)
    return out[None], cache[None]


def solution(mesh):
    n = round(mesh.shape["tok"] ** (1 / 3))
    in_specs = (
        P(None, "tok", None),
        P(),
        P(),
        P(),
        P("section", None, None, None),
        P("section", "tok", None, "fsdp"),
        P("section", "tok", "fsdp"),
        P("section", None, None),
        P("section", None, None, None, "fsdp"),
    )
    out_specs = (P("section", None, "tok", None), P("section", None, None, None, "fsdp"))
    return jax.shard_map(
        functools.partial(local, n), mesh=mesh, in_specs=in_specs, out_specs=out_specs, check_vma=False
    )
```

```python
import functools

import jax
import jax.numpy as jnp
from jax import lax
from jax.experimental import pallas as pl
from jax.experimental.pallas import tpu as pltpu
from jax.sharding import PartitionSpec as P

HEAD_DIM = 64
F32 = jnp.float32
BF16 = jnp.bfloat16
HIDE = -1e30
HID, WA, Z, A, F, X, FIN, MS, RS = range(9)
COPIES = 9
FETCHES = 7


def bits(number):
    assert number & (number - 1) == 0
    return number.bit_length() - 1


def matmul(a, b):
    return jnp.dot(a, b, preferred_element_type=F32)


def matmul_t(a, b):
    return lax.dot_general(a, b, (((1,), (1,)), ((), ())), preferred_element_type=F32)


def pick(index, values):
    out = jnp.zeros(index.shape, jnp.int32)
    for at, value in enumerate(values):
        out = jnp.where(index == at, value, out)
    return out


def relay(n, nf, patches, cd, hid_in, lens_in, text_in, time_in, mod_in, wq_in, wo_in, gain, stale, lo, cache,
          lens, text, time, hid, mine_m, all_m, mine_h, xres, xb, mod_all, mod_in_order, mod, mb, wq, wmine, wbuf, wobuf,
          part_all, part_send, part_recv, total_ref, kv, zb, ab, osum, osend, orecv, ob, fin, cv, stl, old, fetches, sends, recvs, first, second, out_first, out_second, put_sems, gate):
    width = hid.shape[-1]
    rows_w = wq.shape[1]
    local = wq.shape[2]
    hl = local // n
    hc = hl // HEAD_DIM
    groups = n * n
    ranks = nf * n
    out_w = width // ranks
    run = n * cd
    rows = patches * run
    cap = groups * run
    own_rows = patches * cd
    piece = width // groups

    s, f, t = lax.axis_index("section"), lax.axis_index("fsdp"), lax.axis_index("tok")
    x, z, y = t // (n * n), (t // n) % n, t % n
    g = x * n + y
    k = z * nf + f

    def to(x_, z_, y_, f_=None, s_=None):
        return {"section": s if s_ is None else s_, "fsdp": f if f_ is None else f_, "tok": (x_ * n + z_) * n + y_}

    def copy_to(src, dst, send, recv, target):
        return pltpu.make_async_remote_copy(
            src_ref=src, dst_ref=dst, send_sem=send, recv_sem=recv, device_id=target,
            device_id_type=pl.DeviceIdType.MESH)

    def remote(src, dst, which, target):
        return copy_to(src, dst, sends.at[which], recvs.at[which], target)

    def settle(ref, sem):
        pltpu.make_async_copy(ref, ref, sem).wait()

    def sent(ref, which):
        settle(ref, sends.at[which])

    def arrived(ref, which):
        settle(ref, recvs.at[which])

    def loop(low, high, body):
        def step(i, c):
            body(i)
            return c
        lax.fori_loop(low, high, step, 0)

    fetched = [pltpu.make_async_copy(a, b, fetches.at[i]) for i, (a, b) in enumerate(
        ((hid_in, hid), (wq_in, wq), (lens_in, lens), (text_in, text), (time_in, time), (mod_in, mod_all), (stale, stl)))]
    for fetch in fetched:
        fetch.start()

    barrier = pltpu.get_barrier_semaphore()

    def greet(target):
        pl.semaphore_signal(barrier, inc=1, device_id=target, device_id_type=pl.DeviceIdType.MESH)

    def greet_plane(d):
        g_ = (g + d) % groups
        greet(to(g_ // n, z, g_ % n))
    loop(1, groups, greet_plane)

    def greet_ring(d):
        k_ = (k + d) % ranks
        greet(to(x, k_ // nf, y, k_ % nf))
    loop(1, ranks, greet_ring)

    def greet_section(k_):
        greet(to(x, k_ // nf, y, k_ % nf, 1 - s))
    loop(0, ranks, greet_section)

    def greet_planes(j):
        d, z_ = 1 + j // (n - 1), (z + 1 + j % (n - 1)) % n
        greet(to((x + d) % n, z_, y))
        greet(to(x, z_, (y + d) % n))
    loop(0, (n - 1) ** 2, greet_planes)

    r0 = lax.broadcasted_iota(jnp.int32, (rows, rows), 0)
    r1 = lax.broadcasted_iota(jnp.int32, (rows, rows), 1)

    def flipped(r):
        p_, y_, i_ = r >> bits(run), (r >> bits(cd)) & (n - 1), r & (cd - 1)
        return (y_ * patches + p_) * cd + i_

    fetched[1].wait()
    for z_ in range(n):
        for at, part in enumerate((2, 1, 0)):
            wmine[z_, :, at * hl:(at + 1) * hl] = wq[part, :, z_ * hl:(z_ + 1) * hl]

    for at in (0, 2, 3, 4, 5):
        fetched[at].wait()
    length = [lens[p] for p in range(patches)]
    begin = [sum(length[:p], jnp.int32(0)) for p in range(patches)]

    def about(first_z, count):
        row = lax.broadcasted_iota(jnp.int32, (count, 1), 0)
        row_patch = (row >> bits(cd)) & (patches - 1)
        slot = ((x * n + first_z + (row >> bits(own_rows))) * n + y) * cd + (row & (cd - 1))
        return slot < pick(row_patch, length), (pick(row_patch, begin) + slot) < text[0]

    live, is_text = about(0, rows)

    def feature(values, x_, z_):
        return values[:, (x_ * n + z_) * piece:(x_ * n + z_ + 1) * piece]

    steps = mod_all.shape[1]
    chosen = (lax.broadcasted_iota(jnp.int32, (8, steps), 1) == time[0]).astype(BF16)
    for c in range(mod_all.shape[0]):
        values = matmul(chosen, mod_all[c])[0:1]
        mod_in_order[c:c + 1, :] = values
        mod[c:c + 1, :] = jnp.concatenate([feature(values, x_, z_) for z_ in range(n) for x_ in range(n)], axis=1)

    def modulated(values, text_here, table):
        mean = jnp.mean(values, axis=1, keepdims=True)
        centred = values - mean
        spread = jnp.mean(centred * centred, axis=1, keepdims=True)
        normed = centred * lax.rsqrt(spread + 1e-05)
        scale = jnp.where(text_here, table[4:5, :], table[1:2, :])
        shift = jnp.where(text_here, table[3:4, :], table[0:1, :])
        return (normed * (1.0 + scale) + shift).astype(BF16)

    chunk = n * piece
    split = out_w // piece

    @pl.when(s == 0)
    def _():
        states = hid[...].reshape(own_rows, width)
        normed = modulated(states.astype(F32), about(z, own_rows)[1], mod_in_order)
        for x_ in range(n):
            mine_m[x_] = normed[:, x_ * chunk:(x_ + 1) * chunk]
        for f_ in range(nf):
            for z_ in range(n):
                mine_h[f_, z_] = jnp.concatenate(
                    [feature(states, f_ * split + e, z_) for e in range(split)], axis=1)

    pl.semaphore_wait(barrier, groups - 1 + ranks - 1 + ranks + 2 * (n - 1) ** 2)

    def send(d):
        z_ = (z + d) % n
        remote(wmine.at[z_], wbuf.at[z, x, y], WA, to(x, z_, y)).start()
    loop(1, n, send)
    pltpu.make_async_copy(wmine.at[z], wbuf.at[z, x, y], recvs.at[WA]).start()
    put_wo = pltpu.make_async_copy(wo_in, wobuf.at[x, y], fetches.at[FETCHES])
    put_wo.start()

    @pl.when(s == 0)
    def _():
        def send(j):
            x_, z_ = j // n, j % n
            same = (x_ == x) & (z_ == z)

            @pl.when(same)
            def _():
                pltpu.make_async_copy(mine_m.at[x], all_m.at[x * n + z], recvs.at[MS]).start()

            @pl.when(jnp.logical_not(same))
            def _():
                remote(mine_m.at[x_], all_m.at[x * n + z], MS, to(x_, z_, y)).start()
        loop(0, groups, send)

        def send(d):
            z_ = (z + d) % n
            remote(mine_h.at[f, z_], xres.at[z], HID, to(x, z_, y)).start()
        loop(1, n, send)
        pltpu.make_async_copy(mine_h.at[f, z], xres.at[z], recvs.at[HID]).start()

    class Gather:
        def __init__(self, at, block, count):
            self.at, self.block, self.count = at, block, count

        def start(self):
            for half in range(2):
                mine = self.block(half, x, y)

                def send(d, half=half, mine=mine):
                    x_, y_ = (x + d) % n, (y + d) % n
                    along_x, along_y = to(x_, z, y), to(x, z, y_)
                    near, far = (along_x, along_y) if half == 0 else (along_y, along_x)
                    mark = x if half == 0 else y
                    copy_to(mine, mine, out_first.at[self.at, half], first.at[self.at, half, mark], near).start()
                    copy_to(mine, mine, out_second.at[self.at, half], second.at[self.at, half], far).start()
                loop(1, n, send)

        def forward(self):
            for d in range(1, n):
                for half in range(2):
                    mark = ((x if half == 0 else y) + d) % n
                    part = self.block(half, mark, y) if half == 0 else self.block(half, x, mark)
                    settle(part, first.at[self.at, half, mark])

                    def send(e, half=half, part=part):
                        far = to(x, z, (y + e) % n) if half == 0 else to((x + e) % n, z, y)
                        copy_to(part, part, out_second.at[self.at, half], second.at[self.at, half], far).start()
                    loop(1, n, send)

        def wait(self):
            for half in range(2):
                settle(self.count(half, n * (n - 1)), second.at[self.at, half])

        def close(self):
            for half in range(2):
                settle(self.count(half, n - 1), out_first.at[self.at, half])
                settle(self.count(half, n * (n - 1)), out_second.at[self.at, half])

    def count_of(ref, m):
        return ref(pl.ds(0, n), pl.ds(0, n - 1)) if m == n * (n - 1) else ref(0, pl.ds(0, n - 1))

    hz = n // 2
    w_gather = Gather(
        0, lambda half, x_, y_: wbuf.at[pl.ds(half * hz, hz), x_, y_],
        lambda half, m: count_of(lambda a, b: wbuf.at[pl.ds(half * hz, hz), a, b], m))
    wide = local // 2
    o_gather = Gather(
        1, lambda half, x_, y_: wobuf.at[x_, y_, :, pl.ds(half * wide, wide)],
        lambda half, m: count_of(lambda a, b: wobuf.at[a, b, :, pl.ds(half * wide, wide)], m))
    hr = rows // 2
    kv_gather = Gather(
        3, lambda half, x_, y_: kv.at[x_ * n + y_, pl.ds(half * hr, hr)],
        lambda half, m: kv.at[pl.ds(0, m), pl.ds(half * hr, hr)])
    c_gather = Gather(
        2, lambda half, x_, y_: cv.at[half, :, pl.ds(pl.multiple_of((x_ * n + y_) * run, run), run)],
        lambda half, m: cv.at[half, :, pl.ds(0, m * run)])

    arrived(wmine, WA)
    most_w = wbuf.at[:, 0, pl.ds(0, n - 1)]

    @pl.when(s == 0)
    def _():
        def send(d):
            part = wbuf.at[:, x, y]
            copy_to(part, part, out_second.at[0, 0], second.at[0, 0], to(x, z, (y + d) % n)).start()
        loop(1, n, send)
        put_wo.wait()
        o_gather.start()
        arrived(all_m, MS)
        settle(most_w, second.at[0, 0])
        pl.semaphore_signal(gate, 1, device_id=to(x, z, y, f, 1), device_id_type=pl.DeviceIdType.MESH)
        weight = wbuf[:, x].reshape(chunk, 3 * hl)
        parts = matmul(all_m[...].reshape(n * rows, chunk), weight).reshape(n, rows, 3 * hl)
        part_send[...] = parts.astype(BF16)
        part_all[...] = parts

        def send(d):
            x_ = (x + d) % n
            remote(part_send.at[x_], part_recv.at[x], RS, to(x_, z, y)).start()
        loop(1, n, send)
        arrived(part_recv.at[pl.ds(0, n - 1)], RS)
        total = part_all[x]
        for d in range(1, n):
            total = total + part_recv[(x + d) % n].astype(F32)
        total_ref[...] = total

    @pl.when(s == 1)
    def _():
        pl.semaphore_wait(gate, 1)
        w_gather.start()
        put_wo.wait()
        w_gather.forward()
        o_gather.start()
        arrived(xb, X)
        for at in range(n):
            here = slice(at * own_rows, (at + 1) * own_rows)
            values = jnp.concatenate([xb[k_, here, :] for k_ in range(ranks)], axis=1).astype(F32)
            mb[here, :] = modulated(values, about(at, own_rows)[1], mod)
        w_gather.wait()
        total_ref[...] = matmul(mb[...], wbuf[...].reshape(width, 3 * hl))
    total = total_ref[...]

    head = lax.broadcasted_iota(jnp.int32, (1, hl), 1) >> bits(HEAD_DIM)

    def head_norm(values, gains):
        mean = jnp.zeros_like(values)
        for h in range(hc):
            here = head == h
            mean = jnp.where(here, jnp.sum(jnp.where(here, values, 0.0), axis=1, keepdims=True) / HEAD_DIM, mean)
        centred = values - mean
        square = centred * centred
        spread = jnp.zeros_like(values)
        for h in range(hc):
            here = head == h
            spread = jnp.where(here, jnp.sum(jnp.where(here, square, 0.0), axis=1, keepdims=True) / HEAD_DIM, spread)
        return centred * lax.rsqrt(spread + 1e-06) * jnp.concatenate([gains] * hc, axis=1)

    value_new = jnp.where(live, total[:, :hl], 0.0)
    key_new = jnp.where(live, head_norm(total[:, hl:2 * hl], gain[1:2, :]), 0.0)
    kv[g] = jnp.concatenate([value_new, key_new], axis=1).astype(BF16)

    kv_gather.start()

    def send(d):
        own_z, z_ = d // n, d % n
        part = kv.at[g, pl.ds(pl.multiple_of(own_z * own_rows, own_rows), own_rows)]
        same = (own_z == y) & (z_ == z)

        @pl.when(same)
        def _():
            pltpu.make_async_copy(part, zb.at[z * n + y], recvs.at[Z]).start()

        @pl.when(jnp.logical_not(same))
        def _():
            remote(part, zb.at[z * n + y], Z, to(x, z_, own_z)).start()
    loop(0, groups, send)

    query = head_norm(total[:, 2 * hl:], gain[0:1, :])
    query = jnp.concatenate([jnp.zeros((rows, hl), F32), query], axis=1)
    lane = lax.broadcasted_iota(jnp.int32, (1, 2 * hl), 1)
    queries = jnp.concatenate(
        [jnp.where(((lane - hl) >> bits(HEAD_DIM)) == h, query, 0.0) for h in range(hc)], axis=0).astype(BF16)
    query_row = lax.broadcasted_iota(jnp.int32, (hc * rows, 1), 0)
    query_patch = (query_row >> bits(cd)) & (patches - 1)
    column = lax.broadcasted_iota(jnp.int32, (1, patches * cap), 1)

    fetched[6].wait()
    for z_ in range(n):
        @pl.when(z == z_)
        def _(z_=z_):
            mine = slice(z_ * hl, (z_ + 1) * hl)
            both = jnp.concatenate([stl[1, :, :, mine], stl[0, :, :, mine]], axis=2)
            old[...] = both.reshape(patches * cap, 2 * hl)
    old_patch = column >> bits(cap)
    old_seen = ((column & (cap - 1)) < pick(old_patch, length))
    kv_gather.forward()
    score_old = matmul_t(queries, old[...]) * HEAD_DIM ** (-0.5)
    score_old = jnp.where(old_seen & (old_patch > query_patch), score_old, HIDE)
    top_old = jnp.max(score_old, axis=1, keepdims=True)

    o_gather.forward()

    def assemble():
        arrived(zb, Z)
        order = (flipped(r0) == r1).astype(BF16)
        for at, lanes in enumerate((slice(hl, 2 * hl), slice(0, hl))):
            both = jnp.concatenate([zb[z_ * n:(z_ + 1) * n].reshape(rows, 2 * hl)[:, lanes] for z_ in range(n)], axis=1)
            cv[at, :, pl.ds(pl.multiple_of(g * run, run), run), :] = matmul(order, both).astype(BF16).reshape(patches, run, local)
        c_gather.start()

    @pl.when(s == 1)
    def _():
        assemble()

    kv_gather.wait()
    new = kv[...].reshape(patches * cap, 2 * hl)
    new_patch = (column >> bits(cd)) & (patches - 1)
    new_group, new_z = column >> bits(rows), (column >> bits(own_rows)) & (n - 1)
    new_tok = ((new_group >> bits(n)) * n + new_z) * n + (new_group & (n - 1))
    new_slot = new_tok * cd + (column & (cd - 1))
    new_seen = new_slot < pick(new_patch, length)
    score_new = matmul_t(queries, new) * HEAD_DIM ** (-0.5)
    score_new = jnp.where(new_seen & (new_patch <= query_patch), score_new, HIDE)
    top = jnp.maximum(top_old, jnp.max(score_new, axis=1, keepdims=True))
    expo_old, expo_new = jnp.exp(score_old - top), jnp.exp(score_new - top)
    norm = 1.0 / (jnp.sum(expo_old, axis=1, keepdims=True) + jnp.sum(expo_new, axis=1, keepdims=True))
    taken = matmul((expo_old * norm).astype(BF16), old[...]) + matmul((expo_new * norm).astype(BF16), new)
    attended = jnp.zeros((rows, hl), F32)
    for h in range(hc):
        attended = jnp.where(head == h, taken[h * rows:(h + 1) * rows, :hl], attended)
    ab[z] = attended.astype(BF16)

    def send(d):
        remote(ab.at[z], ab.at[z], A, to(x, (z + d) % n, y)).start()
    loop(1, n, send)

    @pl.when(s == 1)
    def _():
        c_gather.forward()

    @pl.when(s == 0)
    def _():
        assemble()

    o_gather.wait()
    arrived(ab.at[pl.ds(0, n - 1)], A)
    left = jnp.concatenate([ab[z_] for z_ in range(n)], axis=1)
    projected = matmul_t(left, wobuf[...].reshape(nf * out_w, local))
    for f_ in range(nf):
        osum[f_] = projected[:, f_ * out_w:(f_ + 1) * out_w]
    osend[...] = osum[1 - f].astype(BF16)
    remote(osend, orecv, F, to(x, z, y, 1 - f)).start()

    arrived(orecv, F)
    projected = osum[f] + orecv[...].astype(F32)
    columns = pl.ds(pl.multiple_of(k * out_w, out_w), out_w)
    gated = jnp.where(is_text, mod[5:6, columns], mod[2:3, columns])

    @pl.when(s == 0)
    def _():
        arrived(xres, HID)
        xb[k] = xres[...].reshape(rows, out_w)
    result = jnp.where(live, xb[k].astype(F32) + gated * projected, 0.0).astype(BF16)
    ob[...] = result

    @pl.when(s == 0)
    def _():
        def send(k_):
            remote(ob, xb.at[k], X, to(x, k_ // nf, y, k_ % nf, 1)).start()
        loop(0, ranks, send)

    def own(z_):
        return ob.at[pl.ds(pl.multiple_of(z_ * own_rows, own_rows), own_rows)]

    def send(d):
        k_ = (k + d) % ranks
        remote(own(k_ // nf), fin.at[k], FIN, to(x, k_ // nf, y, k_ % nf)).start()
    loop(1, ranks, send)
    pltpu.make_async_copy(own(z), fin.at[k], recvs.at[FIN]).start()

    @pl.when(s == 0)
    def _():
        c_gather.forward()
    arrived(fin, FIN)
    natural = [fin[z_ * nf + x_ // split][:, (x_ % split) * piece:(x_ % split + 1) * piece]
               for x_ in range(n) for z_ in range(n)]
    lo[...] = jnp.concatenate(natural, axis=1).reshape(patches, cd, width)
    c_gather.wait()
    puts = [pltpu.make_async_copy(cv.at[c, p], cache.at[c, p], put_sems.at[c, p]) for c in range(2) for p in range(patches)]
    for put in puts:
        put.start()

    sent(wmine.at[pl.ds(0, n - 1)], WA)

    @pl.when(s == 0)
    def _():
        sent(all_m.at[0:groups - 1], MS)
        sent(xres.at[pl.ds(0, n - 1)], HID)
        settle(most_w, out_second.at[0, 0])
        sent(part_send.at[pl.ds(0, n - 1)], RS)
        sent(xb, X)

    @pl.when(s == 1)
    def _():
        w_gather.close()
    o_gather.close()
    c_gather.close()
    kv_gather.close()
    sent(zb.at[0:groups - 1], Z)
    sent(ab.at[pl.ds(0, n - 1)], A)
    sent(osend, F)

    sent(fin.at[pl.ds(0, ranks - 1)], FIN)
    for put in puts:
        put.wait()


def hand_back(out, cache, lo, new_cache, out_v, cache_v, sems):
    parts = [(out, out_v, lo)]
    for c in range(cache.shape[0]):
        for p in range(cache.shape[1]):
            parts.append((cache.at[c, p], cache_v.at[c, p], new_cache.at[c, p]))
    fetches = [pltpu.make_async_copy(a, b, sems.at[0, i]) for i, (a, b, _) in enumerate(parts)]
    puts = [pltpu.make_async_copy(b, c, sems.at[1, i]) for i, (_, b, c) in enumerate(parts)]
    for fetch in fetches:
        fetch.start()
    for fetch, put in zip(fetches, puts):
        fetch.wait()
        put.start()
    for put in puts:
        put.wait()


def local(n, hidden, lengths, text_count, timestep, mod_table, w_qkv, w_out, qk_gain, stale_cache):
    nf = lax.axis_size("fsdp")
    patches, cd, width = hidden.shape
    rows_w, local_width = w_qkv.shape[1], w_qkv.shape[3]
    hl, groups, ranks = local_width // n, n * n, nf * n
    run = n * cd
    rows, out_w, own_rows, cap = patches * run, width // ranks, patches * cd, groups * run
    steps, kinds = mod_table.shape[1:3]
    vmem, anywhere = pl.BlockSpec(memory_space=pltpu.VMEM), pl.BlockSpec(memory_space=pl.ANY)
    out, cache = pl.pallas_call(
        functools.partial(relay, n, nf, patches, cd),
        out_shape=(
            jax.ShapeDtypeStruct((patches, cd, width), BF16),
            jax.ShapeDtypeStruct((2, patches, cap, local_width), BF16),
        ),
        in_specs=[anywhere] * 7 + [vmem, anywhere],
        out_specs=(vmem, anywhere),
        scratch_shapes=[
            pltpu.SMEM((patches,), jnp.int32),
            pltpu.SMEM((1,), jnp.int32),
            pltpu.SMEM((1,), jnp.int32),
            pltpu.VMEM((patches, cd, width), BF16),
            pltpu.VMEM((n, own_rows, width // n), BF16),
            pltpu.VMEM((groups, own_rows, width // n), BF16),
            pltpu.VMEM((nf, n, own_rows, out_w), BF16),
            pltpu.VMEM((n, own_rows, out_w), BF16),
            pltpu.VMEM((ranks, rows, out_w), BF16),
            pltpu.VMEM((kinds, steps, width), BF16),
            pltpu.VMEM((kinds, width), F32),
            pltpu.VMEM((kinds, width), F32),
            pltpu.VMEM((rows, width), BF16),
            pltpu.VMEM((3, rows_w, local_width), BF16),
            pltpu.VMEM((n, rows_w, 3 * hl), BF16),
            pltpu.VMEM((n, n, n, rows_w, 3 * hl), BF16),
            pltpu.VMEM((n, n, rows_w, local_width), BF16),
            pltpu.VMEM((n, rows, 3 * hl), F32),
            pltpu.VMEM((n, rows, 3 * hl), BF16),
            pltpu.VMEM((n, rows, 3 * hl), BF16),
            pltpu.VMEM((rows, 3 * hl), F32),
            pltpu.VMEM((groups, rows, 2 * hl), BF16),
            pltpu.VMEM((groups, own_rows, 2 * hl), BF16),
            pltpu.VMEM((n, rows, hl), BF16),
            pltpu.VMEM((nf, rows, out_w), F32),
            pltpu.VMEM((rows, out_w), BF16),
            pltpu.VMEM((rows, out_w), BF16),
            pltpu.VMEM((rows, out_w), BF16),
            pltpu.VMEM((ranks, own_rows, out_w), BF16),
            pltpu.VMEM((2, patches, cap, local_width), BF16),
            pltpu.VMEM((2, patches, cap, local_width), BF16),
            pltpu.VMEM((patches * cap, 2 * hl), BF16),
            pltpu.SemaphoreType.DMA((FETCHES + 1,)),
            pltpu.SemaphoreType.DMA((COPIES,)),
            pltpu.SemaphoreType.DMA((COPIES,)),
            pltpu.SemaphoreType.DMA((4, 2, n)),
            pltpu.SemaphoreType.DMA((4, 2)),
            pltpu.SemaphoreType.DMA((4, 2)),
            pltpu.SemaphoreType.DMA((4, 2)),
            pltpu.SemaphoreType.DMA((2, patches)),
            pltpu.SemaphoreType.REGULAR,
        ],
        compiler_params=pltpu.CompilerParams(
            collective_id=0, has_side_effects=True, vmem_limit_bytes=62 * 2**20),
    )(hidden, lengths, text_count, timestep, jnp.swapaxes(mod_table[0], 0, 1), jnp.swapaxes(w_qkv[0], 0, 1), w_out[0],
      qk_gain[0], stale_cache[0])
    out, cache = pl.pallas_call(
        hand_back,
        out_shape=(jax.ShapeDtypeStruct(out.shape, BF16), jax.ShapeDtypeStruct(cache.shape, BF16)),
        in_specs=[anywhere] * 2,
        out_specs=(anywhere, anywhere),
        scratch_shapes=[
            pltpu.VMEM(out.shape, BF16),
            pltpu.VMEM(cache.shape, BF16),
            pltpu.SemaphoreType.DMA((2, 1 + 2 * patches)),
        ],
        compiler_params=pltpu.CompilerParams(vmem_limit_bytes=62 * 2**20),
    )(out, cache)
    return out[None], cache[None]


def solution(mesh):
    n = round(mesh.shape["tok"] ** (1 / 3))
    in_specs = (
        P(None, "tok", None),
        P(),
        P(),
        P(),
        P("section", None, None, None),
        P("section", "tok", None, "fsdp"),
        P("section", "tok", "fsdp"),
        P("section", None, None),
        P("section", None, None, None, "fsdp"),
    )
    out_specs = (P("section", None, "tok", None), P("section", None, None, None, "fsdp"))
    return jax.shard_map(
        functools.partial(local, n), mesh=mesh, in_specs=in_specs, out_specs=out_specs, check_vma=False
    )
```

```python
import functools

import jax
import jax.numpy as jnp
from jax import lax
from jax.experimental import pallas as pl
from jax.experimental.pallas import tpu as pltpu
from jax.sharding import PartitionSpec as P

HEAD_DIM = 64
F32 = jnp.float32
BF16 = jnp.bfloat16
HIDE = -1e30
HID, WA, Z, A, F, X, FIN, MS, RS = range(9)
COPIES = 9
FETCHES = 7


def bits(number):
    assert number & (number - 1) == 0
    return number.bit_length() - 1


def matmul(a, b):
    return jnp.dot(a, b, preferred_element_type=F32)


def matmul_t(a, b):
    return lax.dot_general(a, b, (((1,), (1,)), ((), ())), preferred_element_type=F32)


def pick(index, values):
    out = jnp.zeros(index.shape, jnp.int32)
    for at, value in enumerate(values):
        out = jnp.where(index == at, value, out)
    return out


def relay(n, nf, patches, cd, hid_in, lens_in, text_in, time_in, mod_in, wq_in, wo_in, gain, stale, lo, cache,
          lens, text, time, hid, mine_m, all_m, mine_h, xres, xb, mod_all, mod_in_order, mod, mb, wq, wmine, wbuf, wobuf,
          part_all, part_send, part_recv, total_ref, kv, zb, ab, osum, osend, orecv, ob, fin, cv, stl, old, fetches, sends, recvs, first, second, out_first, out_second, put_sems, gate):
    width = hid.shape[-1]
    rows_w = wq.shape[1]
    local = wq.shape[2]
    hl = local // n
    hc = hl // HEAD_DIM
    groups = n * n
    ranks = nf * n
    out_w = width // ranks
    run = n * cd
    rows = patches * run
    cap = groups * run
    own_rows = patches * cd
    piece = width // groups

    s, f, t = lax.axis_index("section"), lax.axis_index("fsdp"), lax.axis_index("tok")
    x, z, y = t // (n * n), (t // n) % n, t % n
    g = x * n + y
    k = z * nf + f

    def to(x_, z_, y_, f_=None, s_=None):
        return {"section": s if s_ is None else s_, "fsdp": f if f_ is None else f_, "tok": (x_ * n + z_) * n + y_}

    def copy_to(src, dst, send, recv, target):
        return pltpu.make_async_remote_copy(
            src_ref=src, dst_ref=dst, send_sem=send, recv_sem=recv, device_id=target,
            device_id_type=pl.DeviceIdType.MESH)

    def remote(src, dst, which, target):
        return copy_to(src, dst, sends.at[which], recvs.at[which], target)

    def settle(ref, sem):
        pltpu.make_async_copy(ref, ref, sem).wait()

    def sent(ref, which):
        settle(ref, sends.at[which])

    def arrived(ref, which):
        settle(ref, recvs.at[which])

    def loop(low, high, body):
        def step(i, c):
            body(i)
            return c
        lax.fori_loop(low, high, step, 0)

    fetched = [pltpu.make_async_copy(a, b, fetches.at[i]) for i, (a, b) in enumerate(
        ((hid_in, hid), (wq_in, wq), (lens_in, lens), (text_in, text), (time_in, time), (mod_in, mod_all), (stale, stl)))]
    for fetch in fetched:
        fetch.start()

    barrier = pltpu.get_barrier_semaphore()

    def greet(target):
        pl.semaphore_signal(barrier, inc=1, device_id=target, device_id_type=pl.DeviceIdType.MESH)

    def greet_plane(d):
        g_ = (g + d) % groups
        greet(to(g_ // n, z, g_ % n))
    loop(1, groups, greet_plane)

    def greet_ring(d):
        k_ = (k + d) % ranks
        greet(to(x, k_ // nf, y, k_ % nf))
    loop(1, ranks, greet_ring)

    def greet_section(k_):
        greet(to(x, k_ // nf, y, k_ % nf, 1 - s))
    loop(0, ranks, greet_section)

    def greet_planes(j):
        d, z_ = 1 + j // (n - 1), (z + 1 + j % (n - 1)) % n
        greet(to((x + d) % n, z_, y))
        greet(to(x, z_, (y + d) % n))
    loop(0, (n - 1) ** 2, greet_planes)

    r0 = lax.broadcasted_iota(jnp.int32, (rows, rows), 0)
    r1 = lax.broadcasted_iota(jnp.int32, (rows, rows), 1)

    def flipped(r):
        p_, y_, i_ = r >> bits(run), (r >> bits(cd)) & (n - 1), r & (cd - 1)
        return (y_ * patches + p_) * cd + i_

    fetched[1].wait()
    for z_ in range(n):
        for at, part in enumerate((2, 1, 0)):
            wmine[z_, :, at * hl:(at + 1) * hl] = wq[part, :, z_ * hl:(z_ + 1) * hl]

    for at in (0, 2, 3, 4, 5):
        fetched[at].wait()
    length = [lens[p] for p in range(patches)]
    begin = [sum(length[:p], jnp.int32(0)) for p in range(patches)]

    def about(first_z, count):
        row = lax.broadcasted_iota(jnp.int32, (count, 1), 0)
        row_patch = (row >> bits(cd)) & (patches - 1)
        slot = ((x * n + first_z + (row >> bits(own_rows))) * n + y) * cd + (row & (cd - 1))
        return slot < pick(row_patch, length), (pick(row_patch, begin) + slot) < text[0]

    live, is_text = about(0, rows)

    def feature(values, x_, z_):
        return values[:, (x_ * n + z_) * piece:(x_ * n + z_ + 1) * piece]

    steps = mod_all.shape[1]
    chosen = (lax.broadcasted_iota(jnp.int32, (8, steps), 1) == time[0]).astype(BF16)
    for c in range(mod_all.shape[0]):
        values = matmul(chosen, mod_all[c])[0:1]
        mod_in_order[c:c + 1, :] = values
        mod[c:c + 1, :] = jnp.concatenate([feature(values, x_, z_) for z_ in range(n) for x_ in range(n)], axis=1)

    def modulated(values, text_here, table):
        mean = jnp.mean(values, axis=1, keepdims=True)
        centred = values - mean
        spread = jnp.mean(centred * centred, axis=1, keepdims=True)
        normed = centred * lax.rsqrt(spread + 1e-05)
        scale = jnp.where(text_here, table[4:5, :], table[1:2, :])
        shift = jnp.where(text_here, table[3:4, :], table[0:1, :])
        return (normed * (1.0 + scale) + shift).astype(BF16)

    chunk = n * piece
    split = out_w // piece

    @pl.when(s == 0)
    def _():
        states = hid[...].reshape(own_rows, width)
        normed = modulated(states.astype(F32), about(z, own_rows)[1], mod_in_order)
        for x_ in range(n):
            mine_m[x_] = normed[:, x_ * chunk:(x_ + 1) * chunk]
        for f_ in range(nf):
            for z_ in range(n):
                mine_h[f_, z_] = jnp.concatenate(
                    [feature(states, f_ * split + e, z_) for e in range(split)], axis=1)

    pl.semaphore_wait(barrier, groups - 1 + ranks - 1 + ranks + 2 * (n - 1) ** 2)

    def send(d):
        z_ = (z + d) % n
        remote(wmine.at[z_], wbuf.at[z, x, y], WA, to(x, z_, y)).start()
    loop(1, n, send)
    pltpu.make_async_copy(wmine.at[z], wbuf.at[z, x, y], recvs.at[WA]).start()
    put_wo = pltpu.make_async_copy(wo_in, wobuf.at[x, y], fetches.at[FETCHES])
    put_wo.start()

    @pl.when(s == 0)
    def _():
        def send(j):
            x_, z_ = j // n, j % n
            same = (x_ == x) & (z_ == z)

            @pl.when(same)
            def _():
                pltpu.make_async_copy(mine_m.at[x], all_m.at[x * n + z], recvs.at[MS]).start()

            @pl.when(jnp.logical_not(same))
            def _():
                remote(mine_m.at[x_], all_m.at[x * n + z], MS, to(x_, z_, y)).start()
        loop(0, groups, send)

        def send(d):
            z_ = (z + d) % n
            remote(mine_h.at[f, z_], xres.at[z], HID, to(x, z_, y)).start()
        loop(1, n, send)
        pltpu.make_async_copy(mine_h.at[f, z], xres.at[z], recvs.at[HID]).start()

    class Gather:
        def __init__(self, at, block, count):
            self.at, self.block, self.count = at, block, count

        def start(self):
            for half in range(2):
                mine = self.block(half, x, y)

                def send(d, half=half, mine=mine):
                    x_, y_ = (x + d) % n, (y + d) % n
                    along_x, along_y = to(x_, z, y), to(x, z, y_)
                    near, far = (along_x, along_y) if half == 0 else (along_y, along_x)
                    mark = x if half == 0 else y
                    copy_to(mine, mine, out_first.at[self.at, half], first.at[self.at, half, mark], near).start()
                    copy_to(mine, mine, out_second.at[self.at, half], second.at[self.at, half], far).start()
                loop(1, n, send)

        def forward(self):
            for d in range(1, n):
                for half in range(2):
                    mark = ((x if half == 0 else y) + d) % n
                    part = self.block(half, mark, y) if half == 0 else self.block(half, x, mark)
                    settle(part, first.at[self.at, half, mark])

                    def send(e, half=half, part=part):
                        far = to(x, z, (y + e) % n) if half == 0 else to((x + e) % n, z, y)
                        copy_to(part, part, out_second.at[self.at, half], second.at[self.at, half], far).start()
                    loop(1, n, send)

        def wait(self):
            for half in range(2):
                settle(self.count(half, n * (n - 1)), second.at[self.at, half])

        def close(self):
            for half in range(2):
                settle(self.count(half, n - 1), out_first.at[self.at, half])
                settle(self.count(half, n * (n - 1)), out_second.at[self.at, half])

    def count_of(ref, m):
        return ref(pl.ds(0, n), pl.ds(0, n - 1)) if m == n * (n - 1) else ref(0, pl.ds(0, n - 1))

    hz = n // 2
    w_gather = Gather(
        0, lambda half, x_, y_: wbuf.at[pl.ds(half * hz, hz), x_, y_],
        lambda half, m: count_of(lambda a, b: wbuf.at[pl.ds(half * hz, hz), a, b], m))
    wide = local // 2
    o_gather = Gather(
        1, lambda half, x_, y_: wobuf.at[x_, y_, :, pl.ds(half * wide, wide)],
        lambda half, m: count_of(lambda a, b: wobuf.at[a, b, :, pl.ds(half * wide, wide)], m))
    hr = rows // 2
    kv_gather = Gather(
        3, lambda half, x_, y_: kv.at[x_ * n + y_, pl.ds(half * hr, hr)],
        lambda half, m: kv.at[pl.ds(0, m), pl.ds(half * hr, hr)])
    c_gather = Gather(
        2, lambda half, x_, y_: cv.at[half, :, pl.ds(pl.multiple_of((x_ * n + y_) * run, run), run)],
        lambda half, m: cv.at[half, :, pl.ds(0, m * run)])

    arrived(wmine, WA)
    most_w = wbuf.at[:, 0, pl.ds(0, n - 1)]

    @pl.when(s == 0)
    def _():
        def send(d):
            part = wbuf.at[:, x, y]
            copy_to(part, part, out_second.at[0, 0], second.at[0, 0], to(x, z, (y + d) % n)).start()
        loop(1, n, send)
        put_wo.wait()
        o_gather.start()
        arrived(all_m, MS)
        settle(most_w, second.at[0, 0])
        pl.semaphore_signal(gate, 1, device_id=to(x, z, y, f, 1), device_id_type=pl.DeviceIdType.MESH)
        weight = wbuf[:, x].reshape(chunk, 3 * hl)
        parts = matmul(all_m[...].reshape(n * rows, chunk), weight).reshape(n, rows, 3 * hl)
        part_send[...] = parts.astype(BF16)
        part_all[...] = parts

        def send(d):
            x_ = (x + d) % n
            remote(part_send.at[x_], part_recv.at[x], RS, to(x_, z, y)).start()
        loop(1, n, send)
        arrived(part_recv.at[pl.ds(0, n - 1)], RS)
        total = part_all[x]
        for d in range(1, n):
            total = total + part_recv[(x + d) % n].astype(F32)
        total_ref[...] = total

    @pl.when(s == 1)
    def _():
        pl.semaphore_wait(gate, 1)
        w_gather.start()
        put_wo.wait()
        w_gather.forward()
        o_gather.start()
        o_gather.forward()
        arrived(xb, X)
        for at in range(n):
            here = slice(at * own_rows, (at + 1) * own_rows)
            values = jnp.concatenate([xb[k_, here, :] for k_ in range(ranks)], axis=1).astype(F32)
            mb[here, :] = modulated(values, about(at, own_rows)[1], mod)
        w_gather.wait()
        total_ref[...] = matmul(mb[...], wbuf[...].reshape(width, 3 * hl))
    total = total_ref[...]

    head = lax.broadcasted_iota(jnp.int32, (1, hl), 1) >> bits(HEAD_DIM)

    def head_norm(values, gains):
        mean = jnp.zeros_like(values)
        for h in range(hc):
            here = head == h
            mean = jnp.where(here, jnp.sum(jnp.where(here, values, 0.0), axis=1, keepdims=True) / HEAD_DIM, mean)
        centred = values - mean
        square = centred * centred
        spread = jnp.zeros_like(values)
        for h in range(hc):
            here = head == h
            spread = jnp.where(here, jnp.sum(jnp.where(here, square, 0.0), axis=1, keepdims=True) / HEAD_DIM, spread)
        return centred * lax.rsqrt(spread + 1e-06) * jnp.concatenate([gains] * hc, axis=1)

    value_new = jnp.where(live, total[:, :hl], 0.0)
    key_new = jnp.where(live, head_norm(total[:, hl:2 * hl], gain[1:2, :]), 0.0)
    kv[g] = jnp.concatenate([value_new, key_new], axis=1).astype(BF16)

    kv_gather.start()

    def send(d):
        own_z, z_ = d // n, d % n
        part = kv.at[g, pl.ds(pl.multiple_of(own_z * own_rows, own_rows), own_rows)]
        same = (own_z == y) & (z_ == z)

        @pl.when(same)
        def _():
            pltpu.make_async_copy(part, zb.at[z * n + y], recvs.at[Z]).start()

        @pl.when(jnp.logical_not(same))
        def _():
            remote(part, zb.at[z * n + y], Z, to(x, z_, own_z)).start()
    loop(0, groups, send)

    query = head_norm(total[:, 2 * hl:], gain[0:1, :])
    query = jnp.concatenate([jnp.zeros((rows, hl), F32), query], axis=1)
    lane = lax.broadcasted_iota(jnp.int32, (1, 2 * hl), 1)
    queries = jnp.concatenate(
        [jnp.where(((lane - hl) >> bits(HEAD_DIM)) == h, query, 0.0) for h in range(hc)], axis=0).astype(BF16)
    query_row = lax.broadcasted_iota(jnp.int32, (hc * rows, 1), 0)
    query_patch = (query_row >> bits(cd)) & (patches - 1)
    column = lax.broadcasted_iota(jnp.int32, (1, patches * cap), 1)

    fetched[6].wait()
    for z_ in range(n):
        @pl.when(z == z_)
        def _(z_=z_):
            mine = slice(z_ * hl, (z_ + 1) * hl)
            both = jnp.concatenate([stl[1, :, :, mine], stl[0, :, :, mine]], axis=2)
            old[...] = both.reshape(patches * cap, 2 * hl)
    old_patch = column >> bits(cap)
    old_seen = ((column & (cap - 1)) < pick(old_patch, length))
    kv_gather.forward()
    score_old = matmul_t(queries, old[...]) * HEAD_DIM ** (-0.5)
    score_old = jnp.where(old_seen & (old_patch > query_patch), score_old, HIDE)
    top_old = jnp.max(score_old, axis=1, keepdims=True)


    @pl.when(s == 0)
    def _():
        o_gather.forward()

    def assemble():
        arrived(zb, Z)
        order = (flipped(r0) == r1).astype(BF16)
        for at, lanes in enumerate((slice(hl, 2 * hl), slice(0, hl))):
            both = jnp.concatenate([zb[z_ * n:(z_ + 1) * n].reshape(rows, 2 * hl)[:, lanes] for z_ in range(n)], axis=1)
            cv[at, :, pl.ds(pl.multiple_of(g * run, run), run), :] = matmul(order, both).astype(BF16).reshape(patches, run, local)
        c_gather.start()

    @pl.when(s == 1)
    def _():
        assemble()

    kv_gather.wait()
    new = kv[...].reshape(patches * cap, 2 * hl)
    new_patch = (column >> bits(cd)) & (patches - 1)
    new_group, new_z = column >> bits(rows), (column >> bits(own_rows)) & (n - 1)
    new_tok = ((new_group >> bits(n)) * n + new_z) * n + (new_group & (n - 1))
    new_slot = new_tok * cd + (column & (cd - 1))
    new_seen = new_slot < pick(new_patch, length)
    score_new = matmul_t(queries, new) * HEAD_DIM ** (-0.5)
    score_new = jnp.where(new_seen & (new_patch <= query_patch), score_new, HIDE)
    top = jnp.maximum(top_old, jnp.max(score_new, axis=1, keepdims=True))
    expo_old, expo_new = jnp.exp(score_old - top), jnp.exp(score_new - top)
    norm = 1.0 / (jnp.sum(expo_old, axis=1, keepdims=True) + jnp.sum(expo_new, axis=1, keepdims=True))
    taken = matmul((expo_old * norm).astype(BF16), old[...]) + matmul((expo_new * norm).astype(BF16), new)
    attended = jnp.zeros((rows, hl), F32)
    for h in range(hc):
        attended = jnp.where(head == h, taken[h * rows:(h + 1) * rows, :hl], attended)
    ab[z] = attended.astype(BF16)

    def send(d):
        remote(ab.at[z], ab.at[z], A, to(x, (z + d) % n, y)).start()
    loop(1, n, send)

    @pl.when(s == 1)
    def _():
        c_gather.forward()

    @pl.when(s == 0)
    def _():
        assemble()

    o_gather.wait()
    arrived(ab.at[pl.ds(0, n - 1)], A)
    left = jnp.concatenate([ab[z_] for z_ in range(n)], axis=1)
    projected = matmul_t(left, wobuf[...].reshape(nf * out_w, local))
    for f_ in range(nf):
        osum[f_] = projected[:, f_ * out_w:(f_ + 1) * out_w]
    osend[...] = osum[1 - f].astype(BF16)
    remote(osend, orecv, F, to(x, z, y, 1 - f)).start()

    arrived(orecv, F)
    projected = osum[f] + orecv[...].astype(F32)
    columns = pl.ds(pl.multiple_of(k * out_w, out_w), out_w)
    gated = jnp.where(is_text, mod[5:6, columns], mod[2:3, columns])

    @pl.when(s == 0)
    def _():
        arrived(xres, HID)
        xb[k] = xres[...].reshape(rows, out_w)
    result = jnp.where(live, xb[k].astype(F32) + gated * projected, 0.0).astype(BF16)
    ob[...] = result

    @pl.when(s == 0)
    def _():
        def send(k_):
            remote(ob, xb.at[k], X, to(x, k_ // nf, y, k_ % nf, 1)).start()
        loop(0, ranks, send)

    def own(z_):
        return ob.at[pl.ds(pl.multiple_of(z_ * own_rows, own_rows), own_rows)]

    def send(d):
        k_ = (k + d) % ranks
        remote(own(k_ // nf), fin.at[k], FIN, to(x, k_ // nf, y, k_ % nf)).start()
    loop(1, ranks, send)
    pltpu.make_async_copy(own(z), fin.at[k], recvs.at[FIN]).start()

    @pl.when(s == 0)
    def _():
        c_gather.forward()
    arrived(fin, FIN)
    natural = [fin[z_ * nf + x_ // split][:, (x_ % split) * piece:(x_ % split + 1) * piece]
               for x_ in range(n) for z_ in range(n)]
    lo[...] = jnp.concatenate(natural, axis=1).reshape(patches, cd, width)
    c_gather.wait()
    puts = [pltpu.make_async_copy(cv.at[c, p], cache.at[c, p], put_sems.at[c, p]) for c in range(2) for p in range(patches)]
    for put in puts:
        put.start()

    sent(wmine.at[pl.ds(0, n - 1)], WA)

    @pl.when(s == 0)
    def _():
        sent(all_m.at[0:groups - 1], MS)
        sent(xres.at[pl.ds(0, n - 1)], HID)
        settle(most_w, out_second.at[0, 0])
        sent(part_send.at[pl.ds(0, n - 1)], RS)
        sent(xb, X)

    @pl.when(s == 1)
    def _():
        w_gather.close()
    o_gather.close()
    c_gather.close()
    kv_gather.close()
    sent(zb.at[0:groups - 1], Z)
    sent(ab.at[pl.ds(0, n - 1)], A)
    sent(osend, F)

    sent(fin.at[pl.ds(0, ranks - 1)], FIN)
    for put in puts:
        put.wait()


def hand_back(out, cache, lo, new_cache, out_v, cache_v, sems):
    parts = [(out, out_v, lo)]
    for c in range(cache.shape[0]):
        for p in range(cache.shape[1]):
            parts.append((cache.at[c, p], cache_v.at[c, p], new_cache.at[c, p]))
    fetches = [pltpu.make_async_copy(a, b, sems.at[0, i]) for i, (a, b, _) in enumerate(parts)]
    puts = [pltpu.make_async_copy(b, c, sems.at[1, i]) for i, (_, b, c) in enumerate(parts)]
    for fetch in fetches:
        fetch.start()
    for fetch, put in zip(fetches, puts):
        fetch.wait()
        put.start()
    for put in puts:
        put.wait()


def local(n, hidden, lengths, text_count, timestep, mod_table, w_qkv, w_out, qk_gain, stale_cache):
    nf = lax.axis_size("fsdp")
    patches, cd, width = hidden.shape
    rows_w, local_width = w_qkv.shape[1], w_qkv.shape[3]
    hl, groups, ranks = local_width // n, n * n, nf * n
    run = n * cd
    rows, out_w, own_rows, cap = patches * run, width // ranks, patches * cd, groups * run
    steps, kinds = mod_table.shape[1:3]
    vmem, anywhere = pl.BlockSpec(memory_space=pltpu.VMEM), pl.BlockSpec(memory_space=pl.ANY)
    out, cache = pl.pallas_call(
        functools.partial(relay, n, nf, patches, cd),
        out_shape=(
            jax.ShapeDtypeStruct((patches, cd, width), BF16),
            jax.ShapeDtypeStruct((2, patches, cap, local_width), BF16),
        ),
        in_specs=[anywhere] * 7 + [vmem, anywhere],
        out_specs=(vmem, anywhere),
        scratch_shapes=[
            pltpu.SMEM((patches,), jnp.int32),
            pltpu.SMEM((1,), jnp.int32),
            pltpu.SMEM((1,), jnp.int32),
            pltpu.VMEM((patches, cd, width), BF16),
            pltpu.VMEM((n, own_rows, width // n), BF16),
            pltpu.VMEM((groups, own_rows, width // n), BF16),
            pltpu.VMEM((nf, n, own_rows, out_w), BF16),
            pltpu.VMEM((n, own_rows, out_w), BF16),
            pltpu.VMEM((ranks, rows, out_w), BF16),
            pltpu.VMEM((kinds, steps, width), BF16),
            pltpu.VMEM((kinds, width), F32),
            pltpu.VMEM((kinds, width), F32),
            pltpu.VMEM((rows, width), BF16),
            pltpu.VMEM((3, rows_w, local_width), BF16),
            pltpu.VMEM((n, rows_w, 3 * hl), BF16),
            pltpu.VMEM((n, n, n, rows_w, 3 * hl), BF16),
            pltpu.VMEM((n, n, rows_w, local_width), BF16),
            pltpu.VMEM((n, rows, 3 * hl), F32),
            pltpu.VMEM((n, rows, 3 * hl), BF16),
            pltpu.VMEM((n, rows, 3 * hl), BF16),
            pltpu.VMEM((rows, 3 * hl), F32),
            pltpu.VMEM((groups, rows, 2 * hl), BF16),
            pltpu.VMEM((groups, own_rows, 2 * hl), BF16),
            pltpu.VMEM((n, rows, hl), BF16),
            pltpu.VMEM((nf, rows, out_w), F32),
            pltpu.VMEM((rows, out_w), BF16),
            pltpu.VMEM((rows, out_w), BF16),
            pltpu.VMEM((rows, out_w), BF16),
            pltpu.VMEM((ranks, own_rows, out_w), BF16),
            pltpu.VMEM((2, patches, cap, local_width), BF16),
            pltpu.VMEM((2, patches, cap, local_width), BF16),
            pltpu.VMEM((patches * cap, 2 * hl), BF16),
            pltpu.SemaphoreType.DMA((FETCHES + 1,)),
            pltpu.SemaphoreType.DMA((COPIES,)),
            pltpu.SemaphoreType.DMA((COPIES,)),
            pltpu.SemaphoreType.DMA((4, 2, n)),
            pltpu.SemaphoreType.DMA((4, 2)),
            pltpu.SemaphoreType.DMA((4, 2)),
            pltpu.SemaphoreType.DMA((4, 2)),
            pltpu.SemaphoreType.DMA((2, patches)),
            pltpu.SemaphoreType.REGULAR,
        ],
        compiler_params=pltpu.CompilerParams(
            collective_id=0, has_side_effects=True, vmem_limit_bytes=62 * 2**20),
    )(hidden, lengths, text_count, timestep, jnp.swapaxes(mod_table[0], 0, 1), jnp.swapaxes(w_qkv[0], 0, 1), w_out[0],
      qk_gain[0], stale_cache[0])
    out, cache = pl.pallas_call(
        hand_back,
        out_shape=(jax.ShapeDtypeStruct(out.shape, BF16), jax.ShapeDtypeStruct(cache.shape, BF16)),
        in_specs=[anywhere] * 2,
        out_specs=(anywhere, anywhere),
        scratch_shapes=[
            pltpu.VMEM(out.shape, BF16),
            pltpu.VMEM(cache.shape, BF16),
            pltpu.SemaphoreType.DMA((2, 1 + 2 * patches)),
        ],
        compiler_params=pltpu.CompilerParams(vmem_limit_bytes=62 * 2**20),
    )(out, cache)
    return out[None], cache[None]


def solution(mesh):
    n = round(mesh.shape["tok"] ** (1 / 3))
    in_specs = (
        P(None, "tok", None),
        P(),
        P(),
        P(),
        P("section", None, None, None),
        P("section", "tok", None, "fsdp"),
        P("section", "tok", "fsdp"),
        P("section", None, None),
        P("section", None, None, None, "fsdp"),
    )
    out_specs = (P("section", None, "tok", None), P("section", None, None, None, "fsdp"))
    return jax.shard_map(
        functools.partial(local, n), mesh=mesh, in_specs=in_specs, out_specs=out_specs, check_vma=False
    )
```
